256 devices in a mesh: dp: 16 (over x, y), tensor: 16 (over z, core).
Axes of the slice: x: 4, y: 4, z: 8, core: 2. Of those that a mesh axis runs over, the one named last changes fastest.
Arguments:
- inputs: bfloat16 [16384, 8192], P('dp', 'tensor'), may hold values from -6 to 6
- output_gradient: bfloat16 [16384, 8192], P(('dp', 'tensor')), may hold values from -6 to 6
- weight: bfloat16 [8192, 8192], P('tensor'), may hold values from -0.0625 to 0.0625
- adapter_down: bfloat16 [32, 64, 8192], P('dp', None, 'tensor'), may hold values from -0.0625 to 0.0625
- adapter_up: bfloat16 [32, 64, 8192], P('dp', None, 'tensor'), may hold values from -0.0625 to 0.0625
- segment_adapter: int32 [128], replicated, may hold values from 0 to 31, as said below
- adapter_slot_map: int32 [32], replicated, may hold values from 0 to 31, as said below
Outputs:
- input_gradient: bfloat16 [16384, 8192], P('dp', 'tensor')
- grad_down: float32 [32, 64, 8192], P('dp', None, 'tensor')
- grad_up: float32 [32, 64, 8192], P('dp', None, 'tensor')
The draws below stay inside these ranges and needn't reach their ends.
Inputs may be any that keep to these rules, and one draw needn't show every extreme that they name: `segment_adapter`: the adapter of slot j is stored on dp index j // 2. The segments of one replica use adapters of exactly 4 dp indices, 2 segments each. `adapter_slot_map`: A permutation of the adapters.
All inputs are finite; a program needn't handle non-finite values.
Results may differ from the reference program's by a relative error of at most 0.0029.
Values may be sent and summed in bfloat16 or wider, within the bound.
A program may use at most 128 MiB of HBM per device.

```python
import jax
import jax.numpy as jnp

MODEL_WIDTH = 8192
ADAPTER_RANK = 64
SEGMENT_TOKENS = 128
ADP_DEV = 2
ADAPTER_COUNT = 32
SEGS = 8
TOKEN_TOTAL = 16384
N_DP = 16


def shuffled_owners(subkey):
    return jax.random.permutation(subkey, N_DP)


def shuffled_segments(subkey):
    return jax.random.permutation(subkey, SEGS)


def layout(key):
    perm_key, owner_key, local_key, order_key = jax.random.split(key, 4)
    adapter_slot_map = jax.random.permutation(perm_key, ADAPTER_COUNT).astype(jnp.int32)
    adapter_of = jnp.argsort(adapter_slot_map).astype(jnp.int32)
    capacity = max(2, SEGS // N_DP)
    orders = jax.vmap(shuffled_owners)(jax.random.split(owner_key, N_DP))
    groups = jnp.arange(SEGS) // capacity
    owner_rows = orders[:, groups]
    within_owner = jax.random.randint(local_key, (N_DP, SEGS), 0, ADP_DEV)
    slot_row_index = owner_rows * ADP_DEV + within_owner
    adapters = adapter_of[slot_row_index]
    shuffle = jax.vmap(shuffled_segments)(jax.random.split(order_key, N_DP))
    adapters = jnp.take_along_axis(adapters, shuffle, axis=1)
    return (adapter_slot_map, adapters.reshape(-1).astype(jnp.int32))


def draw_segment_adapter(key, part):
    return layout(key)[1]


def draw_adapter_slot_map(key, part):
    return layout(key)[0]


def steps_of(key, dims, shards, smallest, top_value):
    factor_of, own = 1.0, jax.random.fold_in(key, 6)
    for axis_at, shards_of in shards:
        heights = jnp.exp(jax.random.uniform(jax.random.fold_in(own, axis_at), (shards_of,), jnp.float32, smallest / len(shards), top_value / len(shards)))
        factor_of = factor_of * jnp.repeat(heights, dims[axis_at] // shards_of).reshape([-1 if axis == axis_at else 1 for axis in range(len(dims))])
    return factor_of


def gaussian(key, extent, width, bound, cuts=(), kind=jnp.bfloat16):
    entries = jax.random.normal(key, extent, jnp.float32) * width
    if len(cuts) > 0:
        entries = steps_of(key, extent, cuts, -0.22, 0.18) * entries
    return jnp.clip(entries, min=-bound, max=bound).astype(kind)


def setup_inputs(seed: int = 0) -> dict:
    keys = jax.random.split(jax.random.key(seed), 8)
    return {
        "inputs": gaussian(keys[0], (TOKEN_TOTAL, MODEL_WIDTH), 1.0, 6.0, ((0, 16), (1, 16))),
        "output_gradient": gaussian(keys[1], (TOKEN_TOTAL, MODEL_WIDTH), 1.0, 6.0, ((0, 256),)),
        "weight": gaussian(keys[2], (MODEL_WIDTH, MODEL_WIDTH), MODEL_WIDTH ** -0.5, 0.0625, ((0, 16),)),
        "adapter_down": gaussian(keys[3], (ADAPTER_COUNT, ADAPTER_RANK, MODEL_WIDTH), MODEL_WIDTH ** -0.5, 0.0625, ((0, 16), (2, 16))),
        "adapter_up": gaussian(keys[4], (ADAPTER_COUNT, ADAPTER_RANK, MODEL_WIDTH), MODEL_WIDTH ** -0.5, 0.0625, ((0, 16), (2, 16))),
        "segment_adapter": draw_segment_adapter(jax.random.fold_in(keys[7], 71), 0),
        "adapter_slot_map": draw_adapter_slot_map(jax.random.fold_in(keys[7], 71), 0),
    }


ADAPTER_SCALE = 0.5


def reference(inputs, output_gradient, weight, adapter_down, adapter_up, segment_adapter, adapter_slot_map):
    slot_row_index = jnp.take(adapter_slot_map, segment_adapter).astype(jnp.int32)
    seg_total = segment_adapter.shape[0]
    segment_down = jnp.take(adapter_down, slot_row_index, axis=0).astype(jnp.float32)
    segment_up = jnp.take(adapter_up, slot_row_index, axis=0).astype(jnp.float32)
    seg_inputs = inputs.reshape(seg_total, SEGMENT_TOKENS, MODEL_WIDTH).astype(jnp.float32)
    seg_grads = output_gradient.reshape(seg_total, SEGMENT_TOKENS, MODEL_WIDTH).astype(jnp.float32)
    down_acts = jnp.einsum('nxd,nrd->nxr', seg_inputs, segment_down)
    up_grads = jnp.einsum('nxd,nrd->nxr', seg_grads, segment_up)
    down_bf = down_acts.astype(jnp.bfloat16).astype(jnp.float32)
    up_halfwidth = up_grads.astype(jnp.bfloat16).astype(jnp.float32)
    frozen_term = jnp.dot(output_gradient, weight.T, preferred_element_type=jnp.float32)
    adapter_term = jnp.einsum('lkb,lbu->lku', up_halfwidth, segment_down).reshape(TOKEN_TOTAL, MODEL_WIDTH)
    input_gradient = (frozen_term + ADAPTER_SCALE * adapter_term).astype(jnp.bfloat16)
    gradient_scale = ADAPTER_SCALE / SEGMENT_TOKENS
    seg_down = gradient_scale * jnp.einsum('nxr,nxd->nrd', up_halfwidth, seg_inputs)
    seg_up = gradient_scale * jnp.einsum('nxr,nxd->nrd', down_bf, seg_grads)
    grad_down = jax.ops.segment_sum(seg_down, slot_row_index, num_segments=ADAPTER_COUNT)
    grad_up = jax.ops.segment_sum(seg_up, slot_row_index, num_segments=ADAPTER_COUNT)
    return input_gradient, grad_down, grad_up
```

```python
import functools

import jax
import jax.numpy as jnp
from jax import lax
from jax.experimental import pallas as pl
from jax.experimental.pallas import tpu as pltpu
from jax.sharding import PartitionSpec as P

MESH = pl.DeviceIdType.MESH
SCALE = 0.5
SEG = 128
NZ = 8
RANK = 64
HALF = 32
NT = (((1,), (1,)), ((), ()))
TN = (((0,), (0,)), ((), ()))
NN = (((1,), (0,)), ((), ()))

FIRST = [(4, 0), (3, 0), (4, 1), (2, 0), (3, 1), (4, 2), (1, 0), (2, 1), (3, 2), (4, 3)]
SECOND = [(r, a) for a in range(3) for r in range(a, -4, -1)] + [(3, 3), (2, 3), (1, 3), (0, 3)]
ROUNDS = FIRST + SECOND
LAST = len(ROUNDS) - 1


def dot(a, b, dims):
    return lax.dot_general(a, b, dims, preferred_element_type=jnp.float32)


def kernel(
    seg_ref, map_ref, x_hbm, g_hbm, w_hbm, fd_hbm, fu_hbm,
    out_ref, gd_ref, gu_ref,
    grads, weight, acts_in, fd, fu, acc,
    part, part_in, chip_part, rank_in, acts, lhs,
    tab0, tab1, tin0, tin1, sum0, sum1, sin0, sin1,
    loc, zr, dr, zs, ds, fr, fs, pr, ps, tr, ts,
):
    dp = lax.axis_index("dp")
    tp = lax.axis_index("tensor")
    z, c = tp // 2, tp % 2
    x, y = dp // 4, dp % 4
    partner = (dp, z * 2 + (1 - c))

    def at_z(zz):
        return (dp, (zz % NZ) * 2 + c)

    def at_x(xx):
        return ((xx % 4) * 4 + y, tp)

    def at_y(yy):
        return (x * 4 + yy % 4, tp)

    def remote(src, dst, send, recv, device):
        return pltpu.make_async_remote_copy(
            src_ref=src, dst_ref=dst, send_sem=send, recv_sem=recv,
            device_id=device, device_id_type=MESH,
        )

    own = []
    for j in range(NZ):
        own.append(pltpu.make_async_copy(
            g_hbm.at[:, pl.ds(j * 1024, 1024)], grads.at[(j * NZ + z) * 2 + c], loc.at[j]))
    own_fd = pltpu.make_async_copy(fd_hbm, fd.at[pl.ds((x * 4 + y) * 2, 2)], loc.at[8])
    own_fu = pltpu.make_async_copy(fu_hbm, fu.at[pl.ds((y * 4 + x) * 2, 2)], loc.at[9])
    load_x = pltpu.make_async_copy(x_hbm, acts_in, loc.at[10])
    load_w = [
        pltpu.make_async_copy(w_hbm.at[:, pl.ds(j * 1024, 1024)], weight.at[j], loc.at[11 + j])
        for j in range(NZ)
    ]
    for cp in own + [own_fd, own_fu, load_x] + load_w:
        cp.start()

    barrier = pltpu.get_barrier_semaphore()
    for d in range(1, NZ):
        pl.semaphore_signal(barrier, inc=1, device_id=at_z(z + d), device_id_type=MESH)
    for d in range(1, 4):
        pl.semaphore_signal(barrier, inc=1, device_id=at_x(x + d), device_id_type=MESH)
        pl.semaphore_signal(barrier, inc=1, device_id=at_y(y + d), device_id_type=MESH)
    pl.semaphore_signal(barrier, inc=1, device_id=partner, device_id_type=MESH)
    pl.semaphore_wait(barrier, 14)

    def zcopy(s, j, zz):
        i = (j * NZ + s) * 2 + c
        return remote(grads.at[i], grads.at[i], zs, zr.at[j * NZ + s], at_z(zz))

    def dcopy(s, j, core):
        i = (j * NZ + s) * 2 + core
        return remote(grads.at[i], grads.at[i], ds, dr.at[j * NZ + s], partner)

    def chunk(way, r, a):
        s = (z - way * a + 2 * NZ) % NZ
        return s, (s + way * r + 2 * NZ) % NZ

    def issue(k):
        r, a = ROUNDS[k]
        if a == 3 and r in (0, 4):
            @pl.when(c == 0)
            def _():
                zcopy(*chunk(1, r, a), z + 1).start()

            @pl.when(c == 1)
            def _():
                zcopy(*chunk(-1, r, a), z + NZ - 1).start()
        else:
            zcopy(*chunk(1, r, a), z + 1).start()
            zcopy(*chunk(-1, r, a), z + NZ - 1).start()

    def retire(k):
        r, a = ROUNDS[k]
        ways = (1,) if a == 3 and r in (0, 4) else (1, -1)
        for way in ways:
            s, j = chunk(way, r, a + 1)
            zcopy(s, j, z + 1).wait_recv()
            dcopy(s, j, c).start()

    def frozen(s, first, count, order):
        def body(n, carry):
            j = order(n)
            dcopy(s, j, 1 - c).wait_recv()
            g = grads[pl.ds((j * NZ + s) * 2, 2)].reshape(SEG, 1024)
            acc[s] += dot(g, weight[j], NT)
            return carry
        lax.fori_loop(first, first + count, body, 0)

    def slot_of(s):
        return map_ref[seg_ref[dp * NZ + s]]

    def finish(s):
        slot = slot_of(s)
        act = acts[1, pl.ds(0, 2), s].reshape(RANK, SEG)
        out = acc[s] + SCALE * dot(act, fd[slot], TN)
        out_ref[pl.ds(pl.multiple_of(s * SEG, SEG), SEG), :] = out.astype(jnp.bfloat16)

    kinds = ((fd, at_y, y, at_x, x), (fu, at_x, x, at_y, y))

    def factors_first(q):
        buf, at1, p1, _, p2 = kinds[q]
        mine = pl.ds((p2 * 4 + p1) * 2, 2)
        return [remote(buf.at[mine], buf.at[mine], fs.at[q], fr.at[q, d - 1], at1(p1 + d)) for d in (1, 2, 3)]

    def factors_second(q):
        buf, _, _, at2, p2 = kinds[q]
        rows = pl.ds(p2 * 8, 8)
        return [remote(buf.at[rows], buf.at[rows], fs.at[q], fr.at[q, 3], at2(p2 + 1)),
                remote(buf.at[rows], buf.at[rows], fs.at[q], fr.at[q, 4], at2(p2 + 3))]

    def factors_third(q):
        buf, _, _, at2, p2 = kinds[q]
        low = pl.ds(((p2 + 3) % 4) * 8, 4)
        high = pl.ds(((p2 + 1) % 4) * 8 + 4, 4)
        return [remote(buf.at[low], buf.at[low], fs.at[q], fr.at[q, 5], at2(p2 + 1)),
                remote(buf.at[high], buf.at[high], fs.at[q], fr.at[q, 6], at2(p2 + 3))]

    def start_all(copies):
        for cp in copies:
            cp.start()

    def await_all(copies):
        for cp in copies:
            cp.wait_recv()

    def project(q):
        def body(s, carry):
            slot = slot_of(s)
            if q == 0:
                t = dot(fd[slot], acts_in[pl.ds(pl.multiple_of(s * SEG, SEG), SEG), :], NT)
            else:
                owner = slot // 2
                row = ((owner % 4) * 4 + owner // 4) * 2 + slot % 2
                cols = pl.ds(pl.multiple_of(c * 512, 512), 512)
                g = grads[pl.ds((z * NZ + s) * 2, 2), :, cols].reshape(SEG, 512)
                t = dot(fu[row], g, NT)
            part[q, 0, s] = t[:HALF]
            part[q, 1, s] = t[HALF:]
            return carry
        lax.fori_loop(0, NZ, body, 0)

    def share_core(q):
        return remote(part.at[q, 1 - c], part_in.at[q], ps.at[q, 0], pr.at[q, 0], partner)

    def share_chips(q):
        return [remote(chip_part.at[q, (z + d) % NZ], rank_in.at[q, d - 1], ps.at[q, 1], pr.at[q, d], at_z(z + d))
                for d in range(1, NZ)]

    def share_acts(q):
        return [remote(acts.at[q, c, z], acts.at[q, c, z], ps.at[q, 2], pr.at[q, 7 + d], at_z(z + d))
                for d in range(1, NZ)]

    def await_acts(q):
        for d in range(1, NZ):
            s = (z + NZ - d) % NZ
            remote(acts.at[q, c, s], acts.at[q, c, s], ps.at[q, 2], pr.at[q, 7 + d], at_z(z + d)).wait_recv()

    def cross_acts(q):
        return remote(acts.at[q, c], acts.at[q, c], ps.at[q, 3], pr.at[q, 15], partner)

    def await_cross(q):
        remote(acts.at[q, 1 - c], acts.at[q, 1 - c], ps.at[q, 3], pr.at[q, 15], partner).wait_recv()

    def reduce_core(q):
        share_core(q).wait_recv()
        chip_part[q] = part[q, c] + part_in[q]
        start_all(share_chips(q))

    def reduce_chips(q):
        await_all(share_chips(q))
        t = chip_part[q, z]
        for d in range(NZ - 1):
            t = t + rank_in[q, d]
        acts[q, c, z] = t.astype(jnp.bfloat16)
        start_all(share_acts(q))

    routes = ((tab0, tin0, sum0, sin0, at_x, x, at_y, y), (tab1, tin1, sum1, sin1, at_y, y, at_x, x))

    def table(q):
        for h in range(2):
            tab = routes[h][0]

            def body(g, carry):
                for s in range(NZ):
                    slot = slot_of(s)
                    v = acts[q, h, s]
                    for i in range(8):
                        a = g * 8 + i if h == 0 else (i // 2) * 8 + g * 2 + i % 2
                        lhs[i * HALF:(i + 1) * HALF, s * SEG:(s + 1) * SEG] = jnp.where(
                            slot == a, v, jnp.zeros_like(v))
                if q == 0:
                    cols = pl.ds(pl.multiple_of(c * 512, 512), 512)
                    rhs = grads[pl.ds(z * NZ * 2, NZ * 2), :, cols].reshape(NZ * SEG, 512)
                else:
                    rhs = acts_in[...]
                t = dot(lhs[...], rhs, NN) * (SCALE / SEG)
                tab[q, g] = t.astype(jnp.bfloat16).reshape(8, HALF, 512)
                return carry
            lax.fori_loop(0, 4, body, 0)
            start_all(table_first(q, h))

    def table_first(q, h):
        tab, tin, _, _, at1, p1, _, _ = routes[h]
        return [remote(tab.at[q, (p1 + d) % 4], tin.at[q, d - 1], ts.at[q, h, 0], tr.at[q, h, d - 1], at1(p1 + d))
                for d in (1, 2, 3)]

    def table_second(q, h):
        _, _, total, sin, _, _, at2, p2 = routes[h]
        return [remote(total.at[q, (p2 + d) % 4], sin.at[q, d - 1], ts.at[q, h, 1], tr.at[q, h, 2 + d], at2(p2 + d))
                for d in (1, 2, 3)]

    def table_sum(q):
        for h in range(2):
            tab, tin, total, _, _, p1, _, _ = routes[h]
            await_all(table_first(q, h))

            def body(n, carry):
                t = tab[q, p1, pl.ds(n * 2, 2)].astype(jnp.float32)
                for d in range(3):
                    t = t + tin[q, d, pl.ds(n * 2, 2)].astype(jnp.float32)
                total[q, n] = t
                return carry
            lax.fori_loop(0, 4, body, 0)
            start_all(table_second(q, h))

    def table_end(q):
        ref = (gu_ref, gd_ref)[q]
        for h in range(2):
            _, _, total, sin, _, _, _, p2 = routes[h]
            await_all(table_second(q, h))
            t = total[q, p2]
            for d in range(3):
                t = t + sin[q, d]
            ref[:, h * HALF:(h + 1) * HALF, :] = t

    def start_own():
        for j in range(NZ):
            dcopy(z, j, c).start()

    def zero():
        acc[...] = jnp.zeros_like(acc)

    def loads_done():
        load_x.wait()
        for cp in load_w:
            cp.wait()

    def forward(s):
        return lambda n: (s + n) % NZ

    def whole(s):
        frozen(s, 0, NZ, forward(s))

    def near(a, way):
        return (z + way * a + NZ) % NZ

    hooks = {
        0: [lambda: own_fd.wait(), lambda: own_fu.wait(), lambda: start_all(factors_first(0)),
            lambda: start_all(factors_first(1)), start_own],
        1: [zero],
        2: [lambda: await_all(factors_first(0)), lambda: await_all(factors_first(1)),
            lambda: start_all(factors_second(0)), lambda: start_all(factors_second(1))],
        3: [loads_done, lambda: whole(z)],
        6: [lambda: await_all(factors_second(0)), lambda: await_all(factors_second(1)),
            lambda: start_all(factors_third(0)), lambda: start_all(factors_third(1))],
        9: [lambda: await_all(factors_third(0)), lambda: project(0), lambda: share_core(0).start()],
        10: [lambda: await_all(factors_third(1)), lambda: reduce_core(0)],
        12: [lambda: own_cols_ready(), lambda: project(1), lambda: share_core(1).start(),
             lambda: reduce_chips(0)],
        13: [lambda: reduce_core(1)],
        14: [lambda: await_acts(0), lambda: cross_acts(0).start()],
        15: [lambda: await_cross(0), lambda: table(0), lambda: reduce_chips(1)],
        17: [lambda: await_acts(1), lambda: cross_acts(1).start(), lambda: frozen_rest(near(1, -1))],
        18: [lambda: await_cross(1), lambda: table(1)],
        19: [lambda: frozen_rest(near(1, 1))],
        20: [lambda: table_sum(0)],
        21: [lambda: finish(z), lambda: finish(near(1, -1)), lambda: finish(near(1, 1))],
        22: [lambda: frozen_rest(near(2, -1))],
        23: [lambda: frozen_rest(near(2, 1))],
        24: [lambda: table_end(0), lambda: table_sum(1)],
        25: [lambda: finish(near(2, -1)), lambda: finish(near(2, 1))],
        28: [lambda: frozen_rest(near(3, -1)), lambda: frozen_rest(near(3, 1)),
             lambda: finish(near(3, -1)), lambda: finish(near(3, 1)), lambda: table_end(1)],
    }

    def own_cols_ready():
        def body(n, carry):
            dcopy((z + n) % NZ, z, 1 - c).wait_recv()
            return carry
        lax.fori_loop(1, NZ, body, 0)

    def frozen_chunk(s, j):
        g = grads[pl.ds((j * NZ + s) * 2, 2)].reshape(SEG, 1024)
        acc[s] += dot(g, weight[j], NT)

    def frozen_rest(s):
        def body(n, carry):
            j = (z + n) % NZ
            dcopy(s, j, 1 - c).wait_recv()
            frozen_chunk(s, j)
            return carry
        frozen_chunk(s, z)
        lax.fori_loop(1, NZ, body, 0)

    for cp in own:
        cp.wait()
    done = 0
    for k in range(len(ROUNDS)):
        lag = 2 if k < len(FIRST) + 2 else 3
        while done <= k - lag:
            retire(done)
            done += 1
        issue(k)
        for hook in hooks.get(k, []):
            hook()
    far = near(4, 1)
    while done < LAST:
        retire(done)
        done += 1

    frozen_chunk(far, z)
    def body(n, carry):
        j = (far + n) % NZ

        @pl.when(j != z)
        def _():
            dcopy(far, j, 1 - c).wait_recv()
            frozen_chunk(far, j)
        return carry
    lax.fori_loop(1, NZ, body, 0)
    retire(LAST)
    dcopy(far, far, 1 - c).wait_recv()
    frozen_chunk(far, far)
    finish(far)

    def drain(ref, sem):
        pltpu.make_async_copy(ref, ref, sem).wait()

    drain(grads.at[pl.ds(0, 56)], zs)
    drain(grads.at[pl.ds(0, 64)], ds)
    for q in range(2):
        drain((fd, fu)[q].at[pl.ds(0, 30)], fs.at[q])
        drain(part_in.at[q], ps.at[q, 0])
        drain(rank_in.at[q], ps.at[q, 1])
        drain(acts.at[q, c, pl.ds(0, 7)], ps.at[q, 2])
        drain(acts.at[q, c], ps.at[q, 3])
        for h in range(2):
            drain(routes[h][1].at[q], ts.at[q, h, 0])
            drain(routes[h][3].at[q], ts.at[q, h, 1])


def on_device(inputs, output_gradient, weight, adapter_down, adapter_up, segment_adapter, adapter_slot_map):
    any_spec = pl.BlockSpec(memory_space=pl.ANY)
    smem = pl.BlockSpec(memory_space=pltpu.SMEM)
    vmem = pl.BlockSpec(memory_space=pltpu.VMEM)
    bf, f32 = jnp.bfloat16, jnp.float32
    dma = pltpu.SemaphoreType.DMA
    out, gd, gu = pl.pallas_call(
        kernel,
        out_shape=(
            jax.ShapeDtypeStruct((1024, 512), bf),
            jax.ShapeDtypeStruct((2, RANK, 512), f32),
            jax.ShapeDtypeStruct((2, RANK, 512), f32),
        ),
        in_specs=[smem, smem] + [any_spec] * 5,
        out_specs=(vmem, vmem, vmem),
        scratch_shapes=[
            pltpu.VMEM((128, 64, 1024), bf),
            pltpu.VMEM((NZ, 512, 1024), bf),
            pltpu.VMEM((1024, 512), bf),
            pltpu.VMEM((32, RANK, 512), bf),
            pltpu.VMEM((32, RANK, 512), bf),
            pltpu.VMEM((NZ, SEG, 512), f32),
            pltpu.VMEM((2, 2, NZ, HALF, SEG), f32),
            pltpu.VMEM((2, NZ, HALF, SEG), f32),
            pltpu.VMEM((2, NZ, HALF, SEG), f32),
            pltpu.VMEM((2, NZ - 1, HALF, SEG), f32),
            pltpu.VMEM((2, 2, NZ, HALF, SEG), bf),
            pltpu.VMEM((256, 1024), bf),
            pltpu.VMEM((2, 4, 8, HALF, 512), bf),
            pltpu.VMEM((2, 4, 8, HALF, 512), bf),
            pltpu.VMEM((2, 3, 8, HALF, 512), bf),
            pltpu.VMEM((2, 3, 8, HALF, 512), bf),
            pltpu.VMEM((2, 4, 2, HALF, 512), f32),
            pltpu.VMEM((2, 4, 2, HALF, 512), f32),
            pltpu.VMEM((2, 3, 2, HALF, 512), f32),
            pltpu.VMEM((2, 3, 2, HALF, 512), f32),
            dma((19,)),
            dma((64,)),
            dma((64,)),
            dma(()),
            dma(()),
            dma((2, 7)),
            dma((2,)),
            dma((2, 16)),
            dma((2, 4)),
            dma((2, 2, 6)),
            dma((2, 2, 2)),
        ],
        compiler_params=pltpu.CompilerParams(
            collective_id=0, has_side_effects=True, vmem_limit_bytes=60 * 1024 * 1024
        ),
    )(segment_adapter, adapter_slot_map, inputs, output_gradient, weight, adapter_down, adapter_up)
    return out, gd, gu


def solution(mesh):
    in_specs = (
        P("dp", "tensor"),
        P(("dp", "tensor"), None),
        P("tensor", None),
        P("dp", None, "tensor"),
        P("dp", None, "tensor"),
        P(),
        P(),
    )
    out_specs = (P("dp", "tensor"), P("dp", None, "tensor"), P("dp", None, "tensor"))
    return jax.shard_map(
        on_device, mesh=mesh, in_specs=in_specs, out_specs=out_specs, check_vma=False
    )
```

```python
import functools

import jax
import jax.numpy as jnp
from jax import lax
from jax.experimental import pallas as pl
from jax.experimental.pallas import tpu as pltpu
from jax.sharding import PartitionSpec as P

MESH = pl.DeviceIdType.MESH
SCALE = 0.5
SEG = 128
NZ = 8
RANK = 64
HALF = 32
NT = (((1,), (1,)), ((), ()))
TN = (((0,), (0,)), ((), ()))
NN = (((1,), (0,)), ((), ()))

FIRST = [(4, 0), (3, 0), (4, 1), (2, 0), (3, 1), (4, 2), (1, 0), (2, 1), (3, 2), (4, 3)]
SECOND = [(r, a) for a in range(3) for r in range(a, -4, -1)] + [(3, 3), (2, 3), (1, 3), (0, 3)]
ROUNDS = FIRST + SECOND
LAST = len(ROUNDS) - 1


def pairs():
    waiting = {o: [(-1, 0)] for o in range(NZ)}
    out = []
    for k, (r, a) in enumerate(ROUNDS):
        for way in (1,) if a == 3 and r in (0, 4) else (1, -1):
            o = way * (r - a - 1) % NZ
            waiting[o].append((k, -way * (a + 1) % NZ))
            if len(waiting[o]) == 2:
                out.append((k, o, waiting[o][0][1], waiting[o][1][1]))
                waiting[o] = []
    return out


PAIRS = pairs()


def dot(a, b, dims):
    return lax.dot_general(a, b, dims, preferred_element_type=jnp.float32)


def kernel(
    seg_ref, map_ref, x_hbm, g_hbm, w_hbm, fd_hbm, fu_hbm,
    out_ref, gd_ref, gu_ref,
    grads, weight, acts_in, fd, fu, acc,
    part, part_in, chip_part, rank_in, acts, lhs,
    tab0, tab1, far0, far1, tin0, tin1, sum0, sum1, sfar0, sfar1, sin0, sin1,
    loc, zr, dr, zs, ds, fr, fs, pr, ps, tr, ts,
):
    dp = lax.axis_index("dp")
    tp = lax.axis_index("tensor")
    z, c = tp // 2, tp % 2
    x, y = dp // 4, dp % 4
    partner = (dp, z * 2 + (1 - c))

    def at_z(zz):
        return (dp, (zz % NZ) * 2 + c)

    def at_x(xx):
        return ((xx % 4) * 4 + y, tp)

    def at_y(yy):
        return (x * 4 + yy % 4, tp)

    def remote(src, dst, send, recv, device):
        return pltpu.make_async_remote_copy(
            src_ref=src, dst_ref=dst, send_sem=send, recv_sem=recv,
            device_id=device, device_id_type=MESH,
        )

    own = []
    for j in range(NZ):
        own.append(pltpu.make_async_copy(
            g_hbm.at[:, pl.ds(j * 1024, 1024)], grads.at[(j * NZ + z) * 2 + c], loc.at[j]))
    own_fd = pltpu.make_async_copy(fd_hbm, fd.at[pl.ds((x * 4 + y) * 2, 2)], loc.at[8])
    own_fu = pltpu.make_async_copy(fu_hbm, fu.at[pl.ds((y * 4 + x) * 2, 2)], loc.at[9])
    load_x = pltpu.make_async_copy(x_hbm, acts_in, loc.at[10])
    load_w = [
        pltpu.make_async_copy(w_hbm.at[:, pl.ds(j * 1024, 1024)], weight.at[j], loc.at[11 + j])
        for j in range(NZ)
    ]
    for cp in own + [own_fd, own_fu, load_x] + load_w:
        cp.start()

    barrier = pltpu.get_barrier_semaphore()
    for d in range(1, NZ):
        pl.semaphore_signal(barrier, inc=1, device_id=at_z(z + d), device_id_type=MESH)
    for d in range(1, 4):
        pl.semaphore_signal(barrier, inc=1, device_id=at_x(x + d), device_id_type=MESH)
        pl.semaphore_signal(barrier, inc=1, device_id=at_y(y + d), device_id_type=MESH)
    pl.semaphore_signal(barrier, inc=1, device_id=partner, device_id_type=MESH)
    pl.semaphore_wait(barrier, 14)

    def zcopy(s, j, zz):
        i = (j * NZ + s) * 2 + c
        return remote(grads.at[i], grads.at[i], zs, zr.at[j * NZ + s], at_z(zz))

    def dcopy(s, j, core):
        i = (j * NZ + s) * 2 + core
        return remote(grads.at[i], grads.at[i], ds, dr.at[j * NZ + s], partner)

    def chunk(way, r, a):
        s = (z - way * a + 2 * NZ) % NZ
        return s, (s + way * r + 2 * NZ) % NZ

    def issue(k):
        r, a = ROUNDS[k]
        if a == 3 and r in (0, 4):
            @pl.when(c == 0)
            def _():
                zcopy(*chunk(1, r, a), z + 1).start()

            @pl.when(c == 1)
            def _():
                zcopy(*chunk(-1, r, a), z + NZ - 1).start()
        else:
            zcopy(*chunk(1, r, a), z + 1).start()
            zcopy(*chunk(-1, r, a), z + NZ - 1).start()

    def retire(k):
        r, a = ROUNDS[k]
        ways = (1,) if a == 3 and r in (0, 4) else (1, -1)
        for way in ways:
            s, j = chunk(way, r, a + 1)
            zcopy(s, j, z + 1).wait_recv()
            dcopy(s, j, c).start()

    def frozen(o, first, second):
        j, s0, s1 = (z + o) % NZ, (z + first) % NZ, (z + second) % NZ
        dcopy(s0, j, 1 - c).wait_recv()
        dcopy(s1, j, 1 - c).wait_recv()
        g0 = grads[pl.ds((j * NZ + s0) * 2, 2)].reshape(SEG, 1024)
        g1 = grads[pl.ds((j * NZ + s1) * 2, 2)].reshape(SEG, 1024)
        t = dot(jnp.concatenate([g0, g1], axis=0), weight[j], NT)
        acc[s0] += t[:SEG]
        acc[s1] += t[SEG:]

    def slot_of(s):
        return map_ref[seg_ref[dp * NZ + s]]

    def adapter_term():
        def body(s, carry):
            act = acts[1, pl.ds(0, 2), s].reshape(RANK, SEG)
            acc[s] += SCALE * dot(act, fd[slot_of(s)], TN)
            return carry
        lax.fori_loop(0, NZ, body, 0)

    def emit(s):
        out_ref[pl.ds(pl.multiple_of(s * SEG, SEG), SEG), :] = acc[s].astype(jnp.bfloat16)

    kinds = ((fd, at_y, y, at_x, x), (fu, at_x, x, at_y, y))

    def fblock(q, row, col, first=0, count=2):
        buf = kinds[q][0]
        return buf.at[pl.ds((row % 4 * 4 + col % 4) * 2 + first, count)]

    def fsend(q, block, sem, device):
        return remote(block, block, fs.at[q], fr.at[q, sem], device)

    def factors_own(q):
        _, at1, p1, _, p2 = kinds[q]
        mine = fblock(q, p2, p1)
        return [fsend(q, mine, 0, at1(p1 + 1)), fsend(q, mine, 1, at1(p1 + 3))]

    def factors_half(q):
        _, at1, p1, _, p2 = kinds[q]
        return [fsend(q, fblock(q, p2, p1 + 3, 0, 1), 2, at1(p1 + 1)),
                fsend(q, fblock(q, p2, p1 + 1, 1, 1), 3, at1(p1 + 3))]

    def factors_row(q, n):
        _, _, p1, at2, p2 = kinds[q]
        block = fblock(q, p2, p1 + (0, 3, 1, 2)[n])
        return [fsend(q, block, 4 + n, at2(p2 + 1)), fsend(q, block, 8 + n, at2(p2 + 3))]

    def factors_on(q, n):
        _, _, p1, at2, p2 = kinds[q]
        row, col, device = ((p2 + 3, p1, p2 + 1), (p2 + 3, p1 + 3, p2 + 1),
                            (p2 + 1, p1 + 1, p2 + 3), (p2 + 1, p1 + 2, p2 + 3))[n]
        return fsend(q, fblock(q, row, col), 12 + n, at2(device))

    def fwait(q, *which):
        for n in which:
            half = n in (2, 3)
            block = fblock(q, 0, 0, 0, 1 if half else 2)
            fsend(q, block, n, partner).wait_recv()

    def factors0():
        for q in range(2):
            start_all(factors_own(q) + factors_row(q, 0))

    def factors1():
        for q in range(2):
            fwait(q, 0, 1)
            start_all(factors_half(q) + factors_row(q, 1) + factors_row(q, 2))

    def factors2():
        for q in range(2):
            fwait(q, 2, 3, 4)
            start_all(factors_row(q, 3) + [factors_on(q, 0)])

    def factors3():
        for q in range(2):
            fwait(q, 5, 10)
            start_all([factors_on(q, 1), factors_on(q, 2)])

    def factors4():
        for q in range(2):
            fwait(q, 11)
            start_all([factors_on(q, 3)])

    def factors5(q):
        fwait(q, 6, 7, 8, 9, 12, 13, 14, 15)

    def start_all(copies):
        for cp in copies:
            cp.start()

    def await_all(copies):
        for cp in copies:
            cp.wait_recv()

    def project(q):
        def body(s, carry):
            slot = slot_of(s)
            if q == 0:
                t = dot(fd[slot], acts_in[pl.ds(pl.multiple_of(s * SEG, SEG), SEG), :], NT)
            else:
                owner = slot // 2
                row = ((owner % 4) * 4 + owner // 4) * 2 + slot % 2
                cols = pl.ds(pl.multiple_of(c * 512, 512), 512)
                g = grads[pl.ds((z * NZ + s) * 2, 2), :, cols].reshape(SEG, 512)
                t = dot(fu[row], g, NT)
            part[q, 0, s] = t[:HALF]
            part[q, 1, s] = t[HALF:]
            return carry
        lax.fori_loop(0, NZ, body, 0)

    def share_core(q):
        return remote(part.at[q, 1 - c], part_in.at[q], ps.at[q, 0], pr.at[q, 0], partner)

    def share_chips(q):
        return [remote(chip_part.at[q, (z + d) % NZ], rank_in.at[q, d - 1], ps.at[q, 1], pr.at[q, d], at_z(z + d))
                for d in range(1, NZ)]

    def share_acts(q):
        return [remote(acts.at[q, c, z], acts.at[q, c, z], ps.at[q, 2], pr.at[q, 7 + d], at_z(z + d))
                for d in range(1, NZ)]

    def await_acts(q):
        for d in range(1, NZ):
            s = (z + NZ - d) % NZ
            remote(acts.at[q, c, s], acts.at[q, c, s], ps.at[q, 2], pr.at[q, 7 + d], at_z(z + d)).wait_recv()

    def cross_acts(q):
        return remote(acts.at[q, c], acts.at[q, c], ps.at[q, 3], pr.at[q, 15], partner)

    def await_cross(q):
        remote(acts.at[q, 1 - c], acts.at[q, 1 - c], ps.at[q, 3], pr.at[q, 15], partner).wait_recv()

    def reduce_core(q):
        share_core(q).wait_recv()
        chip_part[q] = part[q, c] + part_in[q]
        start_all(share_chips(q))

    def reduce_chips(q):
        await_all(share_chips(q))
        t = chip_part[q, z]
        for d in range(NZ - 1):
            t = t + rank_in[q, d]
        acts[q, c, z] = t.astype(jnp.bfloat16)
        start_all(share_acts(q))

    routes = ((tab0, far0, tin0, sum0, sfar0, sin0, at_x, x, at_y, y),
              (tab1, far1, tin1, sum1, sfar1, sin1, at_y, y, at_x, x))

    def table(q):
        for h in range(2):
            tab, p1 = routes[h][0], routes[h][7]

            def body(n, carry):
                g = (p1 + 2 + 3 * n) % 4
                for s in range(NZ):
                    slot = slot_of(s)
                    v = acts[q, h, s]
                    for i in range(8):
                        a = g * 8 + i if h == 0 else (i // 2) * 8 + g * 2 + i % 2
                        lhs[i * HALF:(i + 1) * HALF, s * SEG:(s + 1) * SEG] = jnp.where(
                            slot == a, v, jnp.zeros_like(v))
                if q == 0:
                    cols = pl.ds(pl.multiple_of(c * 512, 512), 512)
                    rhs = grads[pl.ds(z * NZ * 2, NZ * 2), :, cols].reshape(NZ * SEG, 512)
                else:
                    rhs = acts_in[...]
                t = dot(lhs[...], rhs, NN) * (SCALE / SEG)
                tab[q, g] = t.astype(jnp.bfloat16).reshape(8, HALF, 512)

                @pl.when(n == 0)
                def _():
                    start_all(table_a(q, h))
                return carry
            lax.fori_loop(0, 4, body, 0)

    def table_a(q, h):
        tab, far, _, _, _, _, at1, p1, _, _ = routes[h]
        g = (p1 + 2) % 4
        return [remote(tab.at[q, g, pl.ds(0, 4)], far.at[q, 0], ts.at[q, h, 0], tr.at[q, h, 0], at1(p1 + 1)),
                remote(tab.at[q, g, pl.ds(4, 4)], far.at[q, 1], ts.at[q, h, 0], tr.at[q, h, 1], at1(p1 + 3))]

    def table_b(q, h):
        tab, _, tin, _, _, _, at1, p1, _, _ = routes[h]
        return [remote(tab.at[q, (p1 + 1) % 4], tin.at[q, 0], ts.at[q, h, 0], tr.at[q, h, 2], at1(p1 + 1)),
                remote(tab.at[q, (p1 + 3) % 4], tin.at[q, 1], ts.at[q, h, 0], tr.at[q, h, 3], at1(p1 + 3))]

    def table_c(q, h):
        _, _, _, total, sfar, _, _, _, at2, p2 = routes[h]
        g = (p2 + 2) % 4
        return [remote(total.at[q, g, 0], sfar.at[q, 0], ts.at[q, h, 1], tr.at[q, h, 4], at2(p2 + 1)),
                remote(total.at[q, g, 1], sfar.at[q, 1], ts.at[q, h, 1], tr.at[q, h, 5], at2(p2 + 3))]

    def table_d(q, h):
        _, _, _, total, _, sin, _, _, at2, p2 = routes[h]
        return [remote(total.at[q, (p2 + 1) % 4], sin.at[q, 0], ts.at[q, h, 1], tr.at[q, h, 6], at2(p2 + 1)),
                remote(total.at[q, (p2 + 3) % 4], sin.at[q, 1], ts.at[q, h, 1], tr.at[q, h, 7], at2(p2 + 3))]

    def pass_on(q):
        for h in range(2):
            tab, far, p1 = routes[h][0], routes[h][1], routes[h][7]
            send_a, send_b = table_a(q, h), table_b(q, h)
            for way in range(2):
                send_a[way].wait_recv()
                g, half = (p1 + (1, 3)[way]) % 4, pl.ds(way * 4, 4)
                t = tab[q, g, half].astype(jnp.float32) + far[q, way].astype(jnp.float32)
                tab[q, g, half] = t.astype(jnp.bfloat16)
                send_b[way].start()

    def turn(q):
        for h in range(2):
            tab, tin, total, p1, p2 = routes[h][0], routes[h][2], routes[h][3], routes[h][7], routes[h][9]
            await_all(table_b(q, h))

            def body(n, carry):
                g = (p2 + 2 + n) % 4
                rows = pl.ds(g * 2, 2)
                t = tab[q, p1, rows].astype(jnp.float32) + tin[q, 0, rows].astype(jnp.float32)
                total[q, g] = t + tin[q, 1, rows].astype(jnp.float32)
                return carry
            lax.fori_loop(0, 4, body, 0)
            start_all(table_c(q, h))

    def pass_sum(q):
        for h in range(2):
            total, sfar, p2 = routes[h][3], routes[h][4], routes[h][9]
            send_c, send_d = table_c(q, h), table_d(q, h)
            for way in range(2):
                send_c[way].wait_recv()
                g = (p2 + (1, 3)[way]) % 4
                total[q, g, way] += sfar[q, way]
                send_d[way].start()

    def table_end(q):
        ref = (gu_ref, gd_ref)[q]
        for h in range(2):
            total, sin, p2 = routes[h][3], routes[h][5], routes[h][9]
            await_all(table_d(q, h))
            ref[:, h * HALF:(h + 1) * HALF, :] = total[q, p2] + sin[q, 0] + sin[q, 1]

    def start_own():
        for j in range(NZ):
            dcopy(z, j, c).start()

    def zero():
        acc[...] = jnp.zeros_like(acc)

    def loads_done():
        load_x.wait()
        for cp in load_w:
            cp.wait()

    def near(a, way):
        return (z + way * a + NZ) % NZ

    retired, consumed, emitted = [0], [0], []

    def last_use(d):
        return max(k for k, _, s0, s1 in PAIRS if d in (s0, s1))

    def retire_to(k):
        while retired[0] <= k:
            retire(retired[0])
            retired[0] += 1

    def consume_to(k):
        retire_to(k)
        while consumed[0] < len(PAIRS) and PAIRS[consumed[0]][0] <= k:
            frozen(*PAIRS[consumed[0]][1:])
            consumed[0] += 1

    hooks = {
        0: [own_fd.wait, own_fu.wait, factors0, start_own],
        1: [zero],
        2: [loads_done],
        3: [factors1],
        5: [factors2],
        7: [factors3],
        8: [factors4],
        9: [lambda: factors5(0)],
        10: [lambda: project(0), lambda: share_core(0).start(), lambda: factors5(1)],
        11: [lambda: reduce_core(0), lambda: consume_to(9), lambda: project(1), lambda: share_core(1).start()],
        12: [lambda: reduce_core(1)],
        14: [lambda: reduce_chips(0)],
        15: [lambda: reduce_chips(1)],
        17: [lambda: await_acts(0), lambda: cross_acts(0).start()],
        18: [lambda: await_acts(1), lambda: cross_acts(1).start(), lambda: await_cross(0), lambda: table(0)],
        19: [lambda: await_cross(1), lambda: table(1)],
        20: [lambda: pass_on(0), adapter_term],
        21: [lambda: pass_on(1), lambda: None],
        23: [lambda: turn(0), lambda: None],
        24: [lambda: turn(1)],
        25: [lambda: pass_sum(0)],
        26: [lambda: pass_sum(1)],
        27: [lambda: table_end(0)],
        28: [lambda: table_end(1)],
    }

    for cp in own:
        cp.wait()
    for k in range(len(ROUNDS)):
        lag = 2 if k < 17 else 3
        retire_to(k - lag)
        issue(k)
        consume_to(k - lag - 1)
        for hook in hooks.get(k, []):
            hook()
    retire_to(LAST - 2)
    consume_to(LAST - 4)
    for d in (0, 1, 2):
        for way in (1,) if d == 0 else (1, -1):
            if last_use(way * d % NZ) <= LAST - 4:
                emit((z + way * d + NZ) % NZ)
                emitted.append(way * d % NZ)
    retire_to(LAST - 1)
    consume_to(LAST - 2)
    retire_to(LAST)
    consume_to(LAST)
    for d in range(NZ):
        if d not in emitted:
            emit((z + d) % NZ)

    def drain(ref, sem):
        pltpu.make_async_copy(ref, ref, sem).wait()

    drain(grads.at[pl.ds(0, 56)], zs)
    drain(grads.at[pl.ds(0, 64)], ds)
    for q in range(2):
        drain((fd, fu)[q].at[pl.ds(0, 30)], fs.at[q])
        drain(part_in.at[q], ps.at[q, 0])
        drain(rank_in.at[q], ps.at[q, 1])
        drain(acts.at[q, c, pl.ds(0, 7)], ps.at[q, 2])
        drain(acts.at[q, c], ps.at[q, 3])
        for h in range(2):
            drain(routes[h][0].at[q, pl.ds(0, 3)], ts.at[q, h, 0])
            drain(routes[h][3].at[q, pl.ds(0, 3)], ts.at[q, h, 1])


def store(*refs):
    copies = [pltpu.make_async_copy(refs[i], refs[3 + i], refs[6].at[i]) for i in range(3)]
    for cp in copies:
        cp.start()
    for cp in copies:
        cp.wait()


def on_device(inputs, output_gradient, weight, adapter_down, adapter_up, segment_adapter, adapter_slot_map):
    any_spec = pl.BlockSpec(memory_space=pl.ANY)
    smem = pl.BlockSpec(memory_space=pltpu.SMEM)
    vmem = pl.BlockSpec(memory_space=pltpu.VMEM)
    bf, f32 = jnp.bfloat16, jnp.float32
    dma = pltpu.SemaphoreType.DMA
    out, gd, gu = pl.pallas_call(
        kernel,
        out_shape=(
            pltpu.VMEM((1024, 512), bf),
            pltpu.VMEM((2, RANK, 512), f32),
            pltpu.VMEM((2, RANK, 512), f32),
        ),
        in_specs=[smem, smem] + [any_spec] * 5,
        out_specs=(vmem, vmem, vmem),
        scratch_shapes=[
            pltpu.VMEM((128, 64, 1024), bf),
            pltpu.VMEM((NZ, 512, 1024), bf),
            pltpu.VMEM((1024, 512), bf),
            pltpu.VMEM((32, RANK, 512), bf),
            pltpu.VMEM((32, RANK, 512), bf),
            pltpu.VMEM((NZ, SEG, 512), f32),
            pltpu.VMEM((2, 2, NZ, HALF, SEG), f32),
            pltpu.VMEM((2, NZ, HALF, SEG), f32),
            pltpu.VMEM((2, NZ, HALF, SEG), f32),
            pltpu.VMEM((2, NZ - 1, HALF, SEG), f32),
            pltpu.VMEM((2, 2, NZ, HALF, SEG), bf),
            pltpu.VMEM((256, 1024), bf),
            pltpu.VMEM((2, 4, 8, HALF, 512), bf),
            pltpu.VMEM((2, 4, 8, HALF, 512), bf),
            pltpu.VMEM((2, 2, 4, HALF, 512), bf),
            pltpu.VMEM((2, 2, 4, HALF, 512), bf),
            pltpu.VMEM((2, 2, 8, HALF, 512), bf),
            pltpu.VMEM((2, 2, 8, HALF, 512), bf),
            pltpu.VMEM((2, 4, 2, HALF, 512), f32),
            pltpu.VMEM((2, 4, 2, HALF, 512), f32),
            pltpu.VMEM((2, 2, HALF, 512), f32),
            pltpu.VMEM((2, 2, HALF, 512), f32),
            pltpu.VMEM((2, 2, 2, HALF, 512), f32),
            pltpu.VMEM((2, 2, 2, HALF, 512), f32),
            dma((19,)),
            dma((64,)),
            dma((64,)),
            dma(()),
            dma(()),
            dma((2, 16)),
            dma((2,)),
            dma((2, 16)),
            dma((2, 4)),
            dma((2, 2, 8)),
            dma((2, 2, 2)),
        ],
        compiler_params=pltpu.CompilerParams(
            collective_id=0, has_side_effects=True, vmem_limit_bytes=56 * 1024 * 1024
        ),
    )(segment_adapter, adapter_slot_map, inputs, output_gradient, weight, adapter_down, adapter_up)
    return pl.pallas_call(
        store,
        out_shape=(
            jax.ShapeDtypeStruct((1024, 512), bf),
            jax.ShapeDtypeStruct((2, RANK, 512), f32),
            jax.ShapeDtypeStruct((2, RANK, 512), f32),
        ),
        in_specs=[vmem] * 3,
        out_specs=(any_spec,) * 3,
        scratch_shapes=[dma((3,))],
    )(*(pltpu.with_memory_space_constraint(o, pltpu.VMEM) for o in (out, gd, gu)))


def solution(mesh):
    in_specs = (
        P("dp", "tensor"),
        P(("dp", "tensor"), None),
        P("tensor", None),
        P("dp", None, "tensor"),
        P("dp", None, "tensor"),
        P(),
        P(),
    )
    out_specs = (P("dp", "tensor"), P("dp", None, "tensor"), P("dp", None, "tensor"))
    return jax.shard_map(
        on_device, mesh=mesh, in_specs=in_specs, out_specs=out_specs, check_vma=False
    )
```

```python
import functools

import jax
import jax.numpy as jnp
from jax import lax
from jax.experimental import pallas as pl
from jax.experimental.pallas import tpu as pltpu
from jax.sharding import PartitionSpec as P

MESH = pl.DeviceIdType.MESH
SCALE = 0.5
SEG = 128
NZ = 8
RANK = 64
HALF = 32
NT = (((1,), (1,)), ((), ()))
TN = (((0,), (0,)), ((), ()))
NN = (((1,), (0,)), ((), ()))

FIRST = [(4, 0), (3, 0), (4, 1), (2, 0), (3, 1), (4, 2), (1, 0), (2, 1), (3, 2), (4, 3)]
SECOND = [(r, a) for a in range(3) for r in range(a, -4, -1)] + [(3, 3), (2, 3), (1, 3), (0, 3)]
ROUNDS = FIRST + SECOND
LAST = len(ROUNDS) - 1


def pairs():
    waiting = {o: [(-1, 0)] for o in range(NZ)}
    out = []
    for k, (r, a) in enumerate(ROUNDS):
        for way in (1,) if a == 3 and r in (0, 4) else (1, -1):
            o = way * (r - a - 1) % NZ
            waiting[o].append((k, -way * (a + 1) % NZ))
            if len(waiting[o]) == 2:
                out.append((k, o, waiting[o][0][1], waiting[o][1][1]))
                waiting[o] = []
    return out


PAIRS = pairs()


def dot(a, b, dims):
    return lax.dot_general(a, b, dims, preferred_element_type=jnp.float32)


def kernel(
    seg_ref, map_ref, x_hbm, g_hbm, w_hbm, fd_hbm, fu_hbm,
    out_ref, gd_ref, gu_ref,
    grads, weight, acts_in, fd, fu, acc,
    part, part_in, chip_part, rank_in, acts, lhs,
    tab0, tab1, far0, far1, tin0, tin1, sum0, sum1, sfar0, sfar1, sin0, sin1,
    loc, zr, dr, zs, ds, fr, fs, pr, ps, tr, ts,
):
    dp = lax.axis_index("dp")
    tp = lax.axis_index("tensor")
    z, c = tp // 2, tp % 2
    x, y = dp // 4, dp % 4
    partner = (dp, z * 2 + (1 - c))

    def at_z(zz):
        return (dp, (zz % NZ) * 2 + c)

    def at_x(xx):
        return ((xx % 4) * 4 + y, tp)

    def at_y(yy):
        return (x * 4 + yy % 4, tp)

    def remote(src, dst, send, recv, device):
        return pltpu.make_async_remote_copy(
            src_ref=src, dst_ref=dst, send_sem=send, recv_sem=recv,
            device_id=device, device_id_type=MESH,
        )

    own = []
    for j in range(NZ):
        own.append(pltpu.make_async_copy(
            g_hbm.at[:, pl.ds(j * 1024, 1024)], grads.at[(j * NZ + z) * 2 + c], loc.at[j]))
    own_fd = pltpu.make_async_copy(fd_hbm, fd.at[pl.ds((x * 4 + y) * 2, 2)], loc.at[8])
    own_fu = pltpu.make_async_copy(fu_hbm, fu.at[pl.ds((y * 4 + x) * 2, 2)], loc.at[9])
    load_x = pltpu.make_async_copy(x_hbm, acts_in, loc.at[10])
    load_w = [
        pltpu.make_async_copy(w_hbm.at[:, pl.ds(j * 1024, 1024)], weight.at[j], loc.at[11 + j])
        for j in range(NZ)
    ]
    for cp in own + [own_fd, own_fu, load_x] + load_w:
        cp.start()

    barrier = pltpu.get_barrier_semaphore()
    for d in range(1, NZ):
        pl.semaphore_signal(barrier, inc=1, device_id=at_z(z + d), device_id_type=MESH)
    for d in (1, 3):
        pl.semaphore_signal(barrier, inc=1, device_id=at_x(x + d), device_id_type=MESH)
        pl.semaphore_signal(barrier, inc=1, device_id=at_y(y + d), device_id_type=MESH)
    pl.semaphore_signal(barrier, inc=1, device_id=partner, device_id_type=MESH)
    pl.semaphore_wait(barrier, 12)

    def zcopy(s, j, zz):
        i = (j * NZ + s) * 2 + c
        return remote(grads.at[i], grads.at[i], zs, zr.at[j * NZ + s], at_z(zz))

    def last_z(half, way):
        s, j = chunk(way, *ROUNDS[LAST])
        ref = grads.at[(j * NZ + s) * 2 + c, :, pl.ds(half * 512, 512)]
        return remote(ref, ref, zs, zr.at[64 + half], at_z(z + NZ + way))

    def last_d(half, core):
        far = (z + 4) % NZ
        ref = grads.at[(far * NZ + far) * 2 + core, :, pl.ds(half * 512, 512)]
        return remote(ref, ref, ds, dr.at[64 + half], partner)

    def dcopy(s, j, core):
        i = (j * NZ + s) * 2 + core
        return remote(grads.at[i], grads.at[i], ds, dr.at[j * NZ + s], partner)

    def chunk(way, r, a):
        s = (z - way * a + 2 * NZ) % NZ
        return s, (s + way * r + 2 * NZ) % NZ

    def issue(k):
        r, a = ROUNDS[k]
        if k == LAST:
            for core, way in ((0, 1), (1, -1)):
                @pl.when(c == core)
                def _():
                    last_z(0, way).start()
                    last_z(1, way).start()
        elif a == 3 and r in (0, 4):
            @pl.when(c == 0)
            def _():
                zcopy(*chunk(1, r, a), z + 1).start()

            @pl.when(c == 1)
            def _():
                zcopy(*chunk(-1, r, a), z + NZ - 1).start()
        else:
            zcopy(*chunk(1, r, a), z + 1).start()
            zcopy(*chunk(-1, r, a), z + NZ - 1).start()

    def retire(k):
        r, a = ROUNDS[k]
        ways = (1,) if a == 3 and r in (0, 4) else (1, -1)
        for way in ways:
            s, j = chunk(way, r, a + 1)
            zcopy(s, j, z + 1).wait_recv()
            dcopy(s, j, c).start()

    def frozen(o, first, second):
        j, s0, s1 = (z + o) % NZ, (z + first) % NZ, (z + second) % NZ
        dcopy(s0, j, 1 - c).wait_recv()
        dcopy(s1, j, 1 - c).wait_recv()
        g0 = grads[pl.ds((j * NZ + s0) * 2, 2)].reshape(SEG, 1024)
        g1 = grads[pl.ds((j * NZ + s1) * 2, 2)].reshape(SEG, 1024)
        t = dot(jnp.concatenate([g0, g1], axis=0), weight[j], NT)
        acc[s0] += t[:SEG]
        acc[s1] += t[SEG:]

    def slot_of(s):
        return map_ref[seg_ref[dp * NZ + s]]

    def adapter_term():
        def body(s, carry):
            act = acts[1, pl.ds(0, 2), s].reshape(RANK, SEG)
            acc[s] += SCALE * dot(act, fd[slot_of(s)], TN)
            return carry
        lax.fori_loop(0, NZ, body, 0)

    def emit(s):
        out_ref[pl.ds(pl.multiple_of(s * SEG, SEG), SEG), :] = acc[s].astype(jnp.bfloat16)

    kinds = ((fd, at_y, y, at_x, x), (fu, at_x, x, at_y, y))

    def fblock(q, row, col, first=0, count=2):
        buf = kinds[q][0]
        return buf.at[pl.ds((row % 4 * 4 + col % 4) * 2 + first, count)]

    def fsend(q, block, sem, device):
        return remote(block, block, fs.at[q], fr.at[q, sem], device)

    def factors_own(q):
        _, at1, p1, _, p2 = kinds[q]
        mine = fblock(q, p2, p1)
        return [fsend(q, mine, 0, at1(p1 + 1)), fsend(q, mine, 1, at1(p1 + 3))]

    def factors_half(q):
        _, at1, p1, _, p2 = kinds[q]
        return [fsend(q, fblock(q, p2, p1 + 3, 0, 1), 2, at1(p1 + 1)),
                fsend(q, fblock(q, p2, p1 + 1, 1, 1), 3, at1(p1 + 3))]

    def factors_row(q, n):
        _, _, p1, at2, p2 = kinds[q]
        block = fblock(q, p2, p1 + (0, 3, 1, 2)[n])
        return [fsend(q, block, 4 + n, at2(p2 + 1)), fsend(q, block, 8 + n, at2(p2 + 3))]

    def factors_on(q, n):
        _, _, p1, at2, p2 = kinds[q]
        row, col, device = ((p2 + 3, p1, p2 + 1), (p2 + 3, p1 + 3, p2 + 1),
                            (p2 + 1, p1 + 1, p2 + 3), (p2 + 1, p1 + 2, p2 + 3))[n]
        return fsend(q, fblock(q, row, col), 12 + n, at2(device))

    def fwait(q, *which):
        for n in which:
            half = n in (2, 3)
            block = fblock(q, 0, 0, 0, 1 if half else 2)
            fsend(q, block, n, partner).wait_recv()

    def factors0():
        for q in range(2):
            start_all(factors_own(q) + factors_row(q, 0))

    def factors1():
        for q in range(2):
            fwait(q, 0, 1)
            start_all(factors_half(q) + factors_row(q, 1) + factors_row(q, 2))

    def factors2():
        for q in range(2):
            fwait(q, 2, 3, 4)
            start_all(factors_row(q, 3) + [factors_on(q, 0)])

    def factors3():
        for q in range(2):
            fwait(q, 5, 10)
            start_all([factors_on(q, 1), factors_on(q, 2)])

    def factors4():
        for q in range(2):
            fwait(q, 11)
            start_all([factors_on(q, 3)])

    def factors5(q):
        fwait(q, 6, 7, 8, 9, 12, 13, 14, 15)

    def start_all(copies):
        for cp in copies:
            cp.start()

    def await_all(copies):
        for cp in copies:
            cp.wait_recv()

    def project(q):
        def body(s, carry):
            slot = slot_of(s)
            if q == 0:
                t = dot(fd[slot], acts_in[pl.ds(pl.multiple_of(s * SEG, SEG), SEG), :], NT)
            else:
                owner = slot // 2
                row = ((owner % 4) * 4 + owner // 4) * 2 + slot % 2
                cols = pl.ds(pl.multiple_of(c * 512, 512), 512)
                g = grads[pl.ds((z * NZ + s) * 2, 2), :, cols].reshape(SEG, 512)
                t = dot(fu[row], g, NT)
            part[q, 0, s] = t[:HALF]
            part[q, 1, s] = t[HALF:]
            return carry
        lax.fori_loop(0, NZ, body, 0)

    def share_core(q):
        return remote(part.at[q, 1 - c], part_in.at[q], ps.at[q, 0], pr.at[q, 0], partner)

    def share_chips(q):
        return [remote(chip_part.at[q, (z + d) % NZ], rank_in.at[q, d - 1], ps.at[q, 1], pr.at[q, d], at_z(z + d))
                for d in range(1, NZ)]

    def share_acts(q):
        return [remote(acts.at[q, c, z], acts.at[q, c, z], ps.at[q, 2], pr.at[q, 7 + d], at_z(z + d))
                for d in range(1, NZ)]

    def await_acts(q):
        for d in range(1, NZ):
            s = (z + NZ - d) % NZ
            remote(acts.at[q, c, s], acts.at[q, c, s], ps.at[q, 2], pr.at[q, 7 + d], at_z(z + d)).wait_recv()

    def cross_acts(q):
        return remote(acts.at[q, c], acts.at[q, c], ps.at[q, 3], pr.at[q, 15], partner)

    def await_cross(q):
        remote(acts.at[q, 1 - c], acts.at[q, 1 - c], ps.at[q, 3], pr.at[q, 15], partner).wait_recv()

    def reduce_core(q):
        share_core(q).wait_recv()
        chip_part[q] = part[q, c] + part_in[q]
        start_all(share_chips(q))

    def reduce_chips(q):
        await_all(share_chips(q))
        t = chip_part[q, z]
        for d in range(NZ - 1):
            t = t + rank_in[q, d]
        acts[q, c, z] = t.astype(jnp.bfloat16)
        start_all(share_acts(q))

    routes = ((tab0, far0, tin0, sum0, sfar0, sin0, at_x, x, at_y, y),
              (tab1, far1, tin1, sum1, sfar1, sin1, at_y, y, at_x, x))

    def table(q):
        for h in range(2):
            tab, p1 = routes[h][0], routes[h][7]

            def body(n, carry):
                g = (p1 + 2 + 3 * n) % 4
                for s in range(NZ):
                    slot = slot_of(s)
                    v = acts[q, h, s]
                    for i in range(8):
                        a = g * 8 + i if h == 0 else (i // 2) * 8 + g * 2 + i % 2
                        lhs[i * HALF:(i + 1) * HALF, s * SEG:(s + 1) * SEG] = jnp.where(
                            slot == a, v, jnp.zeros_like(v))
                if q == 0:
                    cols = pl.ds(pl.multiple_of(c * 512, 512), 512)
                    rhs = grads[pl.ds(z * NZ * 2, NZ * 2), :, cols].reshape(NZ * SEG, 512)
                else:
                    rhs = acts_in[...]
                t = dot(lhs[...], rhs, NN) * (SCALE / SEG)
                tab[q, g] = t.astype(jnp.bfloat16).reshape(8, HALF, 512)

                @pl.when(n == 0)
                def _():
                    start_all(table_a(q, h))
                return carry
            lax.fori_loop(0, 4, body, 0)

    def table_a(q, h):
        tab, far, _, _, _, _, at1, p1, _, _ = routes[h]
        g = (p1 + 2) % 4
        return [remote(tab.at[q, g, pl.ds(0, 4)], far.at[q, 0], ts.at[q, h, 0], tr.at[q, h, 0], at1(p1 + 1)),
                remote(tab.at[q, g, pl.ds(4, 4)], far.at[q, 1], ts.at[q, h, 0], tr.at[q, h, 1], at1(p1 + 3))]

    def table_b(q, h):
        tab, _, tin, _, _, _, at1, p1, _, _ = routes[h]
        return [remote(tab.at[q, (p1 + 1) % 4], tin.at[q, 0], ts.at[q, h, 0], tr.at[q, h, 2], at1(p1 + 1)),
                remote(tab.at[q, (p1 + 3) % 4], tin.at[q, 1], ts.at[q, h, 0], tr.at[q, h, 3], at1(p1 + 3))]

    def table_c(q, h):
        _, _, _, total, sfar, _, _, _, at2, p2 = routes[h]
        g = (p2 + 2) % 4
        return [remote(total.at[q, g, 0], sfar.at[q, 0], ts.at[q, h, 1], tr.at[q, h, 4], at2(p2 + 1)),
                remote(total.at[q, g, 1], sfar.at[q, 1], ts.at[q, h, 1], tr.at[q, h, 5], at2(p2 + 3))]

    def table_d(q, h):
        _, _, _, total, _, sin, _, _, at2, p2 = routes[h]
        return [remote(total.at[q, (p2 + 1) % 4], sin.at[q, 0], ts.at[q, h, 1], tr.at[q, h, 6], at2(p2 + 1)),
                remote(total.at[q, (p2 + 3) % 4], sin.at[q, 1], ts.at[q, h, 1], tr.at[q, h, 7], at2(p2 + 3))]

    def pass_on(q):
        for h in range(2):
            tab, far, p1 = routes[h][0], routes[h][1], routes[h][7]
            send_a, send_b = table_a(q, h), table_b(q, h)
            for way in range(2):
                send_a[way].wait_recv()
                g, half = (p1 + (1, 3)[way]) % 4, pl.ds(way * 4, 4)
                t = tab[q, g, half].astype(jnp.float32) + far[q, way].astype(jnp.float32)
                tab[q, g, half] = t.astype(jnp.bfloat16)
                send_b[way].start()

    def turn(q):
        for h in range(2):
            tab, tin, total, p1, p2 = routes[h][0], routes[h][2], routes[h][3], routes[h][7], routes[h][9]
            await_all(table_b(q, h))

            def body(n, carry):
                g = (p2 + 2 + n) % 4
                rows = pl.ds(g * 2, 2)
                t = tab[q, p1, rows].astype(jnp.float32) + tin[q, 0, rows].astype(jnp.float32)
                total[q, g] = t + tin[q, 1, rows].astype(jnp.float32)
                return carry
            lax.fori_loop(0, 4, body, 0)
            start_all(table_c(q, h))

    def pass_sum(q):
        for h in range(2):
            total, sfar, p2 = routes[h][3], routes[h][4], routes[h][9]
            send_c, send_d = table_c(q, h), table_d(q, h)
            for way in range(2):
                send_c[way].wait_recv()
                g = (p2 + (1, 3)[way]) % 4
                total[q, g, way] += sfar[q, way]
                send_d[way].start()

    def table_end(q):
        ref = (gu_ref, gd_ref)[q]
        for h in range(2):
            total, sin, p2 = routes[h][3], routes[h][5], routes[h][9]
            await_all(table_d(q, h))
            ref[:, h * HALF:(h + 1) * HALF, :] = total[q, p2] + sin[q, 0] + sin[q, 1]

    def start_own():
        for j in range(NZ):
            dcopy(z, j, c).start()

    def zero():
        acc[...] = jnp.zeros_like(acc)

    def loads_done():
        load_x.wait()
        for cp in load_w:
            cp.wait()

    def near(a, way):
        return (z + way * a + NZ) % NZ

    retired, consumed, emitted = [0], [0], []

    def last_use(d):
        return max(k for k, _, s0, s1 in PAIRS if d in (s0, s1))

    def retire_to(k):
        while retired[0] <= k:
            retire(retired[0])
            retired[0] += 1

    def consume_to(k):
        retire_to(k)
        while consumed[0] < len(PAIRS) and PAIRS[consumed[0]][0] <= k:
            frozen(*PAIRS[consumed[0]][1:])
            consumed[0] += 1

    hooks = {
        0: [own_fd.wait, own_fu.wait, factors0, start_own],
        1: [zero],
        2: [loads_done],
        3: [factors1],
        5: [factors2],
        7: [factors3],
        8: [factors4],
        9: [lambda: factors5(0)],
        10: [lambda: project(0), lambda: share_core(0).start(), lambda: factors5(1)],
        11: [lambda: reduce_core(0), lambda: consume_to(9), lambda: project(1), lambda: share_core(1).start()],
        12: [lambda: reduce_core(1)],
        13: [lambda: reduce_chips(0)],
        15: [lambda: await_acts(0), lambda: cross_acts(0).start(), lambda: reduce_chips(1)],
        16: [lambda: await_cross(0), lambda: table(0)],
        18: [lambda: await_acts(1), lambda: cross_acts(1).start(), lambda: pass_on(0)],
        19: [lambda: await_cross(1), lambda: table(1)],
        20: [adapter_term],
        21: [lambda: pass_on(1), lambda: turn(0)],
        23: [lambda: pass_sum(0)],
        24: [lambda: turn(1)],
        25: [lambda: table_end(0)],
        26: [lambda: pass_sum(1)],
    }

    for cp in own:
        cp.wait()
    for k in range(len(ROUNDS)):
        lag = 2 if k < 10 else 3
        retire_to(k - lag)
        issue(k)
        consume_to(k - lag - 1)
        for hook in hooks.get(k, []):
            hook()
    retire_to(LAST - 2)
    consume_to(LAST - 4)
    for d in (0, 1, 2):
        for way in (1,) if d == 0 else (1, -1):
            if last_use(way * d % NZ) <= LAST - 4:
                emit((z + way * d + NZ) % NZ)
                emitted.append(way * d % NZ)
    retire_to(LAST - 1)
    consume_to(LAST - 2)
    far, others = near(4, 1), PAIRS[-1]
    for half in range(2):
        last_z(half, 1).wait_recv()
        last_d(half, c).start()
    consume_to(LAST - 1)
    for d in range(NZ):
        if d not in emitted and d != 4:
            if d != others[2]:
                emit((z + d) % NZ)
    other = (z + others[2]) % NZ
    table_end(1)
    dcopy(other, far, 1 - c).wait_recv()
    for half in range(2):
        last_d(half, 1 - c).wait_recv()
        cols = pl.ds(half * 512, 512)
        g0 = grads[pl.ds((far * NZ + other) * 2, 2), :, cols].reshape(SEG, 512)
        g1 = grads[pl.ds((far * NZ + far) * 2, 2), :, cols].reshape(SEG, 512)
        t = dot(jnp.concatenate([g0, g1], axis=0), weight[far, :, cols], NT)
        acc[other] += t[:SEG]
        acc[far] += t[SEG:]
    emit(other)
    emit(far)

    def drain(ref, sem):
        pltpu.make_async_copy(ref, ref, sem).wait()

    drain(grads.at[pl.ds(0, 56)], zs)
    drain(grads.at[pl.ds(0, 64)], ds)
    for q in range(2):
        drain((fd, fu)[q].at[pl.ds(0, 30)], fs.at[q])
        drain(part_in.at[q], ps.at[q, 0])
        drain(rank_in.at[q], ps.at[q, 1])
        drain(acts.at[q, c, pl.ds(0, 7)], ps.at[q, 2])
        drain(acts.at[q, c], ps.at[q, 3])
        for h in range(2):
            drain(routes[h][0].at[q, pl.ds(0, 3)], ts.at[q, h, 0])
            drain(routes[h][3].at[q, pl.ds(0, 3)], ts.at[q, h, 1])


def store(*refs):
    copies = [pltpu.make_async_copy(refs[i], refs[3 + i], refs[6].at[i]) for i in range(3)]
    for cp in copies:
        cp.start()
    for cp in copies:
        cp.wait()


def on_device(inputs, output_gradient, weight, adapter_down, adapter_up, segment_adapter, adapter_slot_map):
    any_spec = pl.BlockSpec(memory_space=pl.ANY)
    smem = pl.BlockSpec(memory_space=pltpu.SMEM)
    vmem = pl.BlockSpec(memory_space=pltpu.VMEM)
    bf, f32 = jnp.bfloat16, jnp.float32
    dma = pltpu.SemaphoreType.DMA
    out, gd, gu = pl.pallas_call(
        kernel,
        out_shape=(
            pltpu.VMEM((1024, 512), bf),
            pltpu.VMEM((2, RANK, 512), f32),
            pltpu.VMEM((2, RANK, 512), f32),
        ),
        in_specs=[smem, smem] + [any_spec] * 5,
        out_specs=(vmem, vmem, vmem),
        scratch_shapes=[
            pltpu.VMEM((128, 64, 1024), bf),
            pltpu.VMEM((NZ, 512, 1024), bf),
            pltpu.VMEM((1024, 512), bf),
            pltpu.VMEM((32, RANK, 512), bf),
            pltpu.VMEM((32, RANK, 512), bf),
            pltpu.VMEM((NZ, SEG, 512), f32),
            pltpu.VMEM((2, 2, NZ, HALF, SEG), f32),
            pltpu.VMEM((2, NZ, HALF, SEG), f32),
            pltpu.VMEM((2, NZ, HALF, SEG), f32),
            pltpu.VMEM((2, NZ - 1, HALF, SEG), f32),
            pltpu.VMEM((2, 2, NZ, HALF, SEG), bf),
            pltpu.VMEM((256, 1024), bf),
            pltpu.VMEM((2, 4, 8, HALF, 512), bf),
            pltpu.VMEM((2, 4, 8, HALF, 512), bf),
            pltpu.VMEM((2, 2, 4, HALF, 512), bf),
            pltpu.VMEM((2, 2, 4, HALF, 512), bf),
            pltpu.VMEM((2, 2, 8, HALF, 512), bf),
            pltpu.VMEM((2, 2, 8, HALF, 512), bf),
            pltpu.VMEM((2, 4, 2, HALF, 512), f32),
            pltpu.VMEM((2, 4, 2, HALF, 512), f32),
            pltpu.VMEM((2, 2, HALF, 512), f32),
            pltpu.VMEM((2, 2, HALF, 512), f32),
            pltpu.VMEM((2, 2, 2, HALF, 512), f32),
            pltpu.VMEM((2, 2, 2, HALF, 512), f32),
            dma((19,)),
            dma((66,)),
            dma((66,)),
            dma(()),
            dma(()),
            dma((2, 16)),
            dma((2,)),
            dma((2, 16)),
            dma((2, 4)),
            dma((2, 2, 8)),
            dma((2, 2, 2)),
        ],
        compiler_params=pltpu.CompilerParams(
            collective_id=0, has_side_effects=True, vmem_limit_bytes=56 * 1024 * 1024
        ),
    )(segment_adapter, adapter_slot_map, inputs, output_gradient, weight, adapter_down, adapter_up)
    return pl.pallas_call(
        store,
        out_shape=(
            jax.ShapeDtypeStruct((1024, 512), bf),
            jax.ShapeDtypeStruct((2, RANK, 512), f32),
            jax.ShapeDtypeStruct((2, RANK, 512), f32),
        ),
        in_specs=[vmem] * 3,
        out_specs=(any_spec,) * 3,
        scratch_shapes=[dma((3,))],
    )(*(pltpu.with_memory_space_constraint(o, pltpu.VMEM) for o in (out, gd, gu)))


def solution(mesh):
    in_specs = (
        P("dp", "tensor"),
        P(("dp", "tensor"), None),
        P("tensor", None),
        P("dp", None, "tensor"),
        P("dp", None, "tensor"),
        P(),
        P(),
    )
    out_specs = (P("dp", "tensor"), P("dp", None, "tensor"), P("dp", None, "tensor"))
    return jax.shard_map(
        on_device, mesh=mesh, in_specs=in_specs, out_specs=out_specs, check_vma=False
    )
```

```python
import functools

import jax
import jax.numpy as jnp
from jax import lax
from jax.experimental import pallas as pl
from jax.experimental.pallas import tpu as pltpu
from jax.sharding import PartitionSpec as P

MESH = pl.DeviceIdType.MESH
SCALE = 0.5
SEG = 128
NZ = 8
RANK = 64
HALF = 32
NT = (((1,), (1,)), ((), ()))
TN = (((0,), (0,)), ((), ()))
NN = (((1,), (0,)), ((), ()))

FIRST = [(4, 0), (3, 0), (4, 1), (2, 0), (3, 1), (4, 2), (1, 0), (2, 1), (3, 2), (4, 3)]
SECOND = [(r, a) for a in range(3) for r in range(a, -4, -1)] + [(3, 3), (2, 3), (1, 3), (0, 3)]
ROUNDS = FIRST + SECOND
LAST = len(ROUNDS) - 1


def pairs():
    waiting = {o: [(-1, 0)] for o in range(NZ)}
    out = []
    for k, (r, a) in enumerate(ROUNDS):
        for way in (1,) if a == 3 and r in (0, 4) else (1, -1):
            o = way * (r - a - 1) % NZ
            waiting[o].append((k, -way * (a + 1) % NZ))
            if len(waiting[o]) == 2:
                out.append((k, o, waiting[o][0][1], waiting[o][1][1]))
                waiting[o] = []
    return out


PAIRS = pairs()


def dot(a, b, dims):
    return lax.dot_general(a, b, dims, preferred_element_type=jnp.float32)


def kernel(
    seg_ref, map_ref, x_hbm, g_hbm, w_hbm, fd_hbm, fu_hbm,
    out_ref, gd_ref, gu_ref,
    grads, weight, acts_in, fd, fu, acc,
    part, part_in, chip_part, rank_in, acts, lhs,
    tab0, tab1, far0, far1, tin0, tin1, sum0, sum1, sfar0, sfar1, sin0, sin1,
    loc, zr, dr, zs, ds, fr, fs, pr, ps, tr, ts,
):
    dp = lax.axis_index("dp")
    tp = lax.axis_index("tensor")
    z, c = tp // 2, tp % 2
    x, y = dp // 4, dp % 4
    partner = (dp, z * 2 + (1 - c))

    def at_z(zz):
        return (dp, (zz % NZ) * 2 + c)

    def at_x(xx):
        return ((xx % 4) * 4 + y, tp)

    def at_y(yy):
        return (x * 4 + yy % 4, tp)

    def remote(src, dst, send, recv, device):
        return pltpu.make_async_remote_copy(
            src_ref=src, dst_ref=dst, send_sem=send, recv_sem=recv,
            device_id=device, device_id_type=MESH,
        )

    barrier = pltpu.get_barrier_semaphore()
    for d in range(1, NZ):
        pl.semaphore_signal(barrier, inc=1, device_id=at_z(z + d), device_id_type=MESH)
    for d in (1, 3):
        pl.semaphore_signal(barrier, inc=1, device_id=at_x(x + d), device_id_type=MESH)
        pl.semaphore_signal(barrier, inc=1, device_id=at_y(y + d), device_id_type=MESH)
    pl.semaphore_signal(barrier, inc=1, device_id=partner, device_id_type=MESH)

    own = []
    for n, o in enumerate((4, 3, 5, 2, 6, 1, 7, 0)):
        j = (z + o) % NZ
        cols = pl.ds(pl.multiple_of(j * 1024, 1024), 1024)
        own.append(pltpu.make_async_copy(g_hbm.at[:, cols], grads.at[(j * NZ + z) * 2 + c], loc.at[n]))
    own_fd = pltpu.make_async_copy(fd_hbm, fd.at[pl.ds((x * 4 + y) * 2, 2)], loc.at[8])
    own_fu = pltpu.make_async_copy(fu_hbm, fu.at[pl.ds((y * 4 + x) * 2, 2)], loc.at[9])
    load_x = pltpu.make_async_copy(x_hbm, acts_in, loc.at[10])
    load_w = [
        pltpu.make_async_copy(w_hbm.at[:, pl.ds(j * 1024, 1024)], weight.at[j], loc.at[11 + j])
        for j in range(NZ)
    ]
    for cp in own + [own_fd, own_fu]:
        cp.start()

    pl.semaphore_wait(barrier, 12)

    def zcopy(s, j, zz):
        i = (j * NZ + s) * 2 + c
        return remote(grads.at[i], grads.at[i], zs, zr.at[j * NZ + s], at_z(zz))

    def last_z(half, way):
        s, j = chunk(way, *ROUNDS[LAST])
        ref = grads.at[(j * NZ + s) * 2 + c, :, pl.ds(half * 512, 512)]
        return remote(ref, ref, zs, zr.at[64 + half], at_z(z + NZ + way))

    def last_d(half, core):
        far = (z + 4) % NZ
        ref = grads.at[(far * NZ + far) * 2 + core, :, pl.ds(half * 512, 512)]
        return remote(ref, ref, ds, dr.at[64 + half], partner)

    def dcopy(s, j, core):
        i = (j * NZ + s) * 2 + core
        return remote(grads.at[i], grads.at[i], ds, dr.at[j * NZ + s], partner)

    def chunk(way, r, a):
        s = (z - way * a + 2 * NZ) % NZ
        return s, (s + way * r + 2 * NZ) % NZ

    def issue(k):
        r, a = ROUNDS[k]
        if k == LAST:
            for core, way in ((0, 1), (1, -1)):
                @pl.when(c == core)
                def _():
                    last_z(0, way).start()
                    last_z(1, way).start()
        elif a == 3 and r in (0, 4):
            @pl.when(c == 0)
            def _():
                zcopy(*chunk(1, r, a), z + 1).start()

            @pl.when(c == 1)
            def _():
                zcopy(*chunk(-1, r, a), z + NZ - 1).start()
        else:
            zcopy(*chunk(1, r, a), z + 1).start()
            zcopy(*chunk(-1, r, a), z + NZ - 1).start()

    def retire(k):
        r, a = ROUNDS[k]
        ways = (1,) if a == 3 and r in (0, 4) else (1, -1)
        for way in ways:
            s, j = chunk(way, r, a + 1)
            zcopy(s, j, z + 1).wait_recv()
            dcopy(s, j, c).start()

    def frozen(o, first, second):
        j, s0, s1 = (z + o) % NZ, (z + first) % NZ, (z + second) % NZ
        dcopy(s0, j, 1 - c).wait_recv()
        dcopy(s1, j, 1 - c).wait_recv()
        g0 = grads[pl.ds((j * NZ + s0) * 2, 2)].reshape(SEG, 1024)
        g1 = grads[pl.ds((j * NZ + s1) * 2, 2)].reshape(SEG, 1024)
        t = dot(jnp.concatenate([g0, g1], axis=0), weight[j], NT)
        acc[s0] += t[:SEG]
        acc[s1] += t[SEG:]

    def slot_of(s):
        return map_ref[seg_ref[dp * NZ + s]]

    def adapter_term():
        def body(s, carry):
            act = acts[1, pl.ds(0, 2), s].reshape(RANK, SEG)
            acc[s] += SCALE * dot(act, fd[slot_of(s)], TN)
            return carry
        lax.fori_loop(0, NZ, body, 0)

    def emit(s):
        out_ref[pl.ds(pl.multiple_of(s * SEG, SEG), SEG), :] = acc[s].astype(jnp.bfloat16)

    kinds = ((fd, at_y, y, at_x, x), (fu, at_x, x, at_y, y))

    def fblock(q, row, col, first=0, count=2):
        buf = kinds[q][0]
        return buf.at[pl.ds((row % 4 * 4 + col % 4) * 2 + first, count)]

    def fsend(q, block, sem, device):
        return remote(block, block, fs.at[q], fr.at[q, sem], device)

    def factors_own(q):
        _, at1, p1, _, p2 = kinds[q]
        mine = fblock(q, p2, p1)
        return [fsend(q, mine, 0, at1(p1 + 1)), fsend(q, mine, 1, at1(p1 + 3))]

    def factors_half(q):
        _, at1, p1, _, p2 = kinds[q]
        return [fsend(q, fblock(q, p2, p1 + 3, 0, 1), 2, at1(p1 + 1)),
                fsend(q, fblock(q, p2, p1 + 1, 1, 1), 3, at1(p1 + 3))]

    def factors_row(q, n):
        _, _, p1, at2, p2 = kinds[q]
        block = fblock(q, p2, p1 + (0, 3, 1, 2)[n])
        return [fsend(q, block, 4 + n, at2(p2 + 1)), fsend(q, block, 8 + n, at2(p2 + 3))]

    def factors_on(q, n):
        _, _, p1, at2, p2 = kinds[q]
        row, col, device = ((p2 + 3, p1, p2 + 1), (p2 + 3, p1 + 3, p2 + 1),
                            (p2 + 1, p1 + 1, p2 + 3), (p2 + 1, p1 + 2, p2 + 3))[n]
        return fsend(q, fblock(q, row, col), 12 + n, at2(device))

    def fwait(q, *which):
        for n in which:
            half = n in (2, 3)
            block = fblock(q, 0, 0, 0, 1 if half else 2)
            fsend(q, block, n, partner).wait_recv()

    def factors0():
        for q in range(2):
            start_all(factors_own(q) + factors_row(q, 0))

    def factors1():
        for q in range(2):
            fwait(q, 0, 1)
            start_all(factors_half(q) + factors_row(q, 1) + factors_row(q, 2))

    def factors2():
        for q in range(2):
            fwait(q, 2, 3, 4)
            start_all(factors_row(q, 3) + [factors_on(q, 0)])

    def factors3():
        for q in range(2):
            fwait(q, 5, 10)
            start_all([factors_on(q, 1), factors_on(q, 2)])

    def factors4():
        for q in range(2):
            fwait(q, 11)
            start_all([factors_on(q, 3)])

    def factors5(q):
        fwait(q, 6, 7, 8, 9, 12, 13, 14, 15)

    def start_all(copies):
        for cp in copies:
            cp.start()

    def await_all(copies):
        for cp in copies:
            cp.wait_recv()

    def project(q):
        def body(s, carry):
            slot = slot_of(s)
            if q == 0:
                t = dot(fd[slot], acts_in[pl.ds(pl.multiple_of(s * SEG, SEG), SEG), :], NT)
            else:
                owner = slot // 2
                row = ((owner % 4) * 4 + owner // 4) * 2 + slot % 2
                cols = pl.ds(pl.multiple_of(c * 512, 512), 512)
                g = grads[pl.ds((z * NZ + s) * 2, 2), :, cols].reshape(SEG, 512)
                t = dot(fu[row], g, NT)
            part[q, 0, s] = t[:HALF]
            part[q, 1, s] = t[HALF:]
            return carry
        lax.fori_loop(0, NZ, body, 0)

    def share_core(q):
        return remote(part.at[q, 1 - c], part_in.at[q], ps.at[q, 0], pr.at[q, 0], partner)

    def share_chips(q):
        return [remote(chip_part.at[q, (z + d) % NZ], rank_in.at[q, d - 1], ps.at[q, 1], pr.at[q, d], at_z(z + d))
                for d in range(1, NZ)]

    def share_acts(q):
        return [remote(acts.at[q, c, z], acts.at[q, c, z], ps.at[q, 2], pr.at[q, 7 + d], at_z(z + d))
                for d in range(1, NZ)]

    def await_acts(q):
        for d in range(1, NZ):
            s = (z + NZ - d) % NZ
            remote(acts.at[q, c, s], acts.at[q, c, s], ps.at[q, 2], pr.at[q, 7 + d], at_z(z + d)).wait_recv()

    def cross_acts(q):
        return remote(acts.at[q, c], acts.at[q, c], ps.at[q, 3], pr.at[q, 15], partner)

    def await_cross(q):
        remote(acts.at[q, 1 - c], acts.at[q, 1 - c], ps.at[q, 3], pr.at[q, 15], partner).wait_recv()

    def reduce_core(q):
        share_core(q).wait_recv()
        chip_part[q] = part[q, c] + part_in[q]
        start_all(share_chips(q))

    def reduce_chips(q):
        await_all(share_chips(q))
        t = chip_part[q, z]
        for d in range(NZ - 1):
            t = t + rank_in[q, d]
        acts[q, c, z] = t.astype(jnp.bfloat16)
        start_all(share_acts(q))

    routes = ((tab0, far0, tin0, sum0, sfar0, sin0, at_x, x, at_y, y),
              (tab1, far1, tin1, sum1, sfar1, sin1, at_y, y, at_x, x))

    def table(q):
        for h in range(2):
            tab, p1 = routes[h][0], routes[h][7]

            def body(n, carry):
                g = (p1 + 2 + 3 * n) % 4
                for s in range(NZ):
                    slot = slot_of(s)
                    v = acts[q, h, s]
                    for i in range(8):
                        a = g * 8 + i if h == 0 else (i // 2) * 8 + g * 2 + i % 2
                        lhs[i * HALF:(i + 1) * HALF, s * SEG:(s + 1) * SEG] = jnp.where(
                            slot == a, v, jnp.zeros_like(v))
                if q == 0:
                    cols = pl.ds(pl.multiple_of(c * 512, 512), 512)
                    rhs = grads[pl.ds(z * NZ * 2, NZ * 2), :, cols].reshape(NZ * SEG, 512)
                else:
                    rhs = acts_in[...]
                t = dot(lhs[...], rhs, NN) * (SCALE / SEG)
                tab[q, g] = t.astype(jnp.bfloat16).reshape(8, HALF, 512)

                @pl.when(n == 0)
                def _():
                    start_all(table_a(q, h))
                return carry
            lax.fori_loop(0, 4, body, 0)

    def table_a(q, h):
        tab, far, _, _, _, _, at1, p1, _, _ = routes[h]
        g = (p1 + 2) % 4
        return [remote(tab.at[q, g, pl.ds(0, 4)], far.at[q, 0], ts.at[q, h, 0], tr.at[q, h, 0], at1(p1 + 1)),
                remote(tab.at[q, g, pl.ds(4, 4)], far.at[q, 1], ts.at[q, h, 0], tr.at[q, h, 1], at1(p1 + 3))]

    def table_b(q, h):
        tab, _, tin, _, _, _, at1, p1, _, _ = routes[h]
        return [remote(tab.at[q, (p1 + 1) % 4], tin.at[q, 0], ts.at[q, h, 0], tr.at[q, h, 2], at1(p1 + 1)),
                remote(tab.at[q, (p1 + 3) % 4], tin.at[q, 1], ts.at[q, h, 0], tr.at[q, h, 3], at1(p1 + 3))]

    def table_c(q, h):
        _, _, _, total, sfar, _, _, _, at2, p2 = routes[h]
        g = (p2 + 2) % 4
        return [remote(total.at[q, g, 0], sfar.at[q, 0], ts.at[q, h, 1], tr.at[q, h, 4], at2(p2 + 1)),
                remote(total.at[q, g, 1], sfar.at[q, 1], ts.at[q, h, 1], tr.at[q, h, 5], at2(p2 + 3))]

    def table_d(q, h):
        _, _, _, total, _, sin, _, _, at2, p2 = routes[h]
        return [remote(total.at[q, (p2 + 1) % 4], sin.at[q, 0], ts.at[q, h, 1], tr.at[q, h, 6], at2(p2 + 1)),
                remote(total.at[q, (p2 + 3) % 4], sin.at[q, 1], ts.at[q, h, 1], tr.at[q, h, 7], at2(p2 + 3))]

    def pass_on(q):
        for h in range(2):
            tab, far, p1 = routes[h][0], routes[h][1], routes[h][7]
            send_a, send_b = table_a(q, h), table_b(q, h)
            for way in range(2):
                send_a[way].wait_recv()
                g, half = (p1 + (1, 3)[way]) % 4, pl.ds(way * 4, 4)
                t = tab[q, g, half].astype(jnp.float32) + far[q, way].astype(jnp.float32)
                tab[q, g, half] = t.astype(jnp.bfloat16)
                send_b[way].start()

    def turn(q):
        for h in range(2):
            tab, tin, total, p1, p2 = routes[h][0], routes[h][2], routes[h][3], routes[h][7], routes[h][9]
            await_all(table_b(q, h))

            def body(n, carry):
                g = (p2 + 2 + n) % 4
                rows = pl.ds(g * 2, 2)
                t = tab[q, p1, rows].astype(jnp.float32) + tin[q, 0, rows].astype(jnp.float32)
                total[q, g] = t + tin[q, 1, rows].astype(jnp.float32)
                return carry
            lax.fori_loop(0, 4, body, 0)
            start_all(table_c(q, h))

    def pass_sum(q):
        for h in range(2):
            total, sfar, p2 = routes[h][3], routes[h][4], routes[h][9]
            send_c, send_d = table_c(q, h), table_d(q, h)
            for way in range(2):
                send_c[way].wait_recv()
                g = (p2 + (1, 3)[way]) % 4
                total[q, g, way] += sfar[q, way]
                send_d[way].start()

    def table_end(q):
        ref = (gu_ref, gd_ref)[q]
        for h in range(2):
            total, sin, p2 = routes[h][3], routes[h][5], routes[h][9]
            await_all(table_d(q, h))
            ref[:, h * HALF:(h + 1) * HALF, :] = total[q, p2] + sin[q, 0] + sin[q, 1]

    def start_own():
        for j in range(NZ):
            dcopy(z, j, c).start()

    def zero():
        acc[...] = jnp.zeros_like(acc)

    def loads_done():
        load_x.wait()
        for cp in load_w:
            cp.wait()

    def near(a, way):
        return (z + way * a + NZ) % NZ

    retired, consumed, emitted = [0], [0], []

    def last_use(d):
        return max(k for k, _, s0, s1 in PAIRS if d in (s0, s1))

    def retire_to(k):
        while retired[0] <= k:
            retire(retired[0])
            retired[0] += 1

    def consume_to(k):
        retire_to(k)
        while consumed[0] < len(PAIRS) and PAIRS[consumed[0]][0] <= k:
            frozen(*PAIRS[consumed[0]][1:])
            consumed[0] += 1

    def rest_own():
        for cp in own[3:]:
            cp.wait()

    hooks = {
        0: [own_fd.wait, own_fu.wait, factors0, own[1].wait, own[2].wait],
        1: [lambda: start_all([load_x] + load_w), rest_own, start_own, zero],
        2: [loads_done],
        3: [factors1],
        5: [factors2],
        7: [factors3],
        8: [factors4],
        9: [lambda: factors5(0)],
        10: [lambda: project(0), lambda: share_core(0).start(), lambda: factors5(1)],
        11: [lambda: reduce_core(0), lambda: consume_to(9), lambda: project(1), lambda: share_core(1).start()],
        12: [lambda: reduce_core(1)],
        13: [lambda: reduce_chips(0)],
        15: [lambda: await_acts(0), lambda: cross_acts(0).start(), lambda: reduce_chips(1)],
        16: [lambda: await_cross(0), lambda: table(0)],
        18: [lambda: await_acts(1), lambda: cross_acts(1).start(), lambda: pass_on(0)],
        19: [lambda: await_cross(1), lambda: table(1)],
        20: [adapter_term],
        21: [lambda: pass_on(1), lambda: turn(0)],
        23: [lambda: pass_sum(0)],
        24: [lambda: turn(1)],
        25: [lambda: table_end(0)],
        26: [lambda: pass_sum(1)],
    }

    own[0].wait()
    for k in range(len(ROUNDS)):
        lag = 2 if k < 10 else 3
        retire_to(k - lag)
        issue(k)
        consume_to(k - lag - 1)
        for hook in hooks.get(k, []):
            hook()
    retire_to(LAST - 2)
    consume_to(LAST - 4)
    for d in (0, 1, 2):
        for way in (1,) if d == 0 else (1, -1):
            if last_use(way * d % NZ) <= LAST - 4:
                emit((z + way * d + NZ) % NZ)
                emitted.append(way * d % NZ)
    retire_to(LAST - 1)
    consume_to(LAST - 2)
    far, others = near(4, 1), PAIRS[-1]
    for half in range(2):
        last_z(half, 1).wait_recv()
        last_d(half, c).start()
    consume_to(LAST - 1)
    for d in range(NZ):
        if d not in emitted and d != 4:
            if d != others[2]:
                emit((z + d) % NZ)
    other = (z + others[2]) % NZ
    table_end(1)
    dcopy(other, far, 1 - c).wait_recv()
    for half in range(2):
        last_d(half, 1 - c).wait_recv()
        cols = pl.ds(half * 512, 512)
        g0 = grads[pl.ds((far * NZ + other) * 2, 2), :, cols].reshape(SEG, 512)
        g1 = grads[pl.ds((far * NZ + far) * 2, 2), :, cols].reshape(SEG, 512)
        t = dot(jnp.concatenate([g0, g1], axis=0), weight[far, :, cols], NT)
        acc[other] += t[:SEG]
        acc[far] += t[SEG:]
    emit(other)
    emit(far)

    def drain(ref, sem):
        pltpu.make_async_copy(ref, ref, sem).wait()

    drain(grads.at[pl.ds(0, 56)], zs)
    drain(grads.at[pl.ds(0, 64)], ds)
    for q in range(2):
        drain((fd, fu)[q].at[pl.ds(0, 30)], fs.at[q])
        drain(part_in.at[q], ps.at[q, 0])
        drain(rank_in.at[q], ps.at[q, 1])
        drain(acts.at[q, c, pl.ds(0, 7)], ps.at[q, 2])
        drain(acts.at[q, c], ps.at[q, 3])
        for h in range(2):
            drain(routes[h][0].at[q, pl.ds(0, 3)], ts.at[q, h, 0])
            drain(routes[h][3].at[q, pl.ds(0, 3)], ts.at[q, h, 1])


def store(*refs):
    copies = [pltpu.make_async_copy(refs[i], refs[3 + i], refs[6].at[i]) for i in range(3)]
    for cp in copies:
        cp.start()
    for cp in copies:
        cp.wait()


def on_device(inputs, output_gradient, weight, adapter_down, adapter_up, segment_adapter, adapter_slot_map):
    any_spec = pl.BlockSpec(memory_space=pl.ANY)
    smem = pl.BlockSpec(memory_space=pltpu.SMEM)
    vmem = pl.BlockSpec(memory_space=pltpu.VMEM)
    bf, f32 = jnp.bfloat16, jnp.float32
    dma = pltpu.SemaphoreType.DMA
    out, gd, gu = pl.pallas_call(
        kernel,
        out_shape=(
            pltpu.VMEM((1024, 512), bf),
            pltpu.VMEM((2, RANK, 512), f32),
            pltpu.VMEM((2, RANK, 512), f32),
        ),
        in_specs=[smem, smem] + [any_spec] * 5,
        out_specs=(vmem, vmem, vmem),
        scratch_shapes=[
            pltpu.VMEM((128, 64, 1024), bf),
            pltpu.VMEM((NZ, 512, 1024), bf),
            pltpu.VMEM((1024, 512), bf),
            pltpu.VMEM((32, RANK, 512), bf),
            pltpu.VMEM((32, RANK, 512), bf),
            pltpu.VMEM((NZ, SEG, 512), f32),
            pltpu.VMEM((2, 2, NZ, HALF, SEG), f32),
            pltpu.VMEM((2, NZ, HALF, SEG), f32),
            pltpu.VMEM((2, NZ, HALF, SEG), f32),
            pltpu.VMEM((2, NZ - 1, HALF, SEG), f32),
            pltpu.VMEM((2, 2, NZ, HALF, SEG), bf),
            pltpu.VMEM((256, 1024), bf),
            pltpu.VMEM((2, 4, 8, HALF, 512), bf),
            pltpu.VMEM((2, 4, 8, HALF, 512), bf),
            pltpu.VMEM((2, 2, 4, HALF, 512), bf),
            pltpu.VMEM((2, 2, 4, HALF, 512), bf),
            pltpu.VMEM((2, 2, 8, HALF, 512), bf),
            pltpu.VMEM((2, 2, 8, HALF, 512), bf),
            pltpu.VMEM((2, 4, 2, HALF, 512), f32),
            pltpu.VMEM((2, 4, 2, HALF, 512), f32),
            pltpu.VMEM((2, 2, HALF, 512), f32),
            pltpu.VMEM((2, 2, HALF, 512), f32),
            pltpu.VMEM((2, 2, 2, HALF, 512), f32),
            pltpu.VMEM((2, 2, 2, HALF, 512), f32),
            dma((19,)),
            dma((66,)),
            dma((66,)),
            dma(()),
            dma(()),
            dma((2, 16)),
            dma((2,)),
            dma((2, 16)),
            dma((2, 4)),
            dma((2, 2, 8)),
            dma((2, 2, 2)),
        ],
        compiler_params=pltpu.CompilerParams(
            collective_id=0, has_side_effects=True, vmem_limit_bytes=56 * 1024 * 1024
        ),
    )(segment_adapter, adapter_slot_map, inputs, output_gradient, weight, adapter_down, adapter_up)
    return pl.pallas_call(
        store,
        out_shape=(
            jax.ShapeDtypeStruct((1024, 512), bf),
            jax.ShapeDtypeStruct((2, RANK, 512), f32),
            jax.ShapeDtypeStruct((2, RANK, 512), f32),
        ),
        in_specs=[vmem] * 3,
        out_specs=(any_spec,) * 3,
        scratch_shapes=[dma((3,))],
    )(*(pltpu.with_memory_space_constraint(o, pltpu.VMEM) for o in (out, gd, gu)))


def solution(mesh):
    in_specs = (
        P("dp", "tensor"),
        P(("dp", "tensor"), None),
        P("tensor", None),
        P("dp", None, "tensor"),
        P("dp", None, "tensor"),
        P(),
        P(),
    )
    out_specs = (P("dp", "tensor"), P("dp", None, "tensor"), P("dp", None, "tensor"))
    return jax.shard_map(
        on_device, mesh=mesh, in_specs=in_specs, out_specs=out_specs, check_vma=False
    )
```
